128 devices in a mesh: seq: 32 (over z, x, core), ch: 4 (over y).
Axes of the slice: x: 4, y: 4, z: 4, core: 2. Of those that a mesh axis runs over, the one named last changes fastest.
Arguments:
- qkv: bfloat16 [3, 16384, 4096], P(None, 'seq', 'ch'), may hold values from -6 to 6
- short_weight: float32 [3, 3, 4096], P(None, None, 'ch'), may hold values from -3.5 to 3.5
- long_filter: float32 [16384, 4096], P('seq', 'ch'), may hold values from -0.125 to 0.125
- skip: float32 [4096], P('ch'), may hold values from -4 to 4
Outputs:
- mixed: bfloat16 [16384, 4096], P('seq', 'ch')
The draws below stay inside these ranges and needn't reach their ends.
All inputs are finite; a program needn't handle non-finite values.
Results may differ from the reference program's by a relative error of at most 0.013.
Values may be sent and summed in bfloat16 or wider, within the bound.
A program may use at most 128 MiB of HBM per device.

```python
import jax
import jax.numpy as jnp
from jax import lax

C = 4096
TOK_DEV = 512
L = 16384
N_SEQ = 32


def levels(stream_key, dims, split, smallest, high):
    gain = 1.0
    for dim, parts in split:
        steps = jax.random.uniform(jax.random.fold_in(jax.random.fold_in(stream_key, 6), dim), (parts,), jnp.float32, smallest / len(split), high / len(split))
        gain = gain * jnp.repeat(jnp.exp(steps), dims[dim] // parts).reshape((-1,) + (1,) * (len(dims) - 1 - dim))
    return gain


def gaussian(own_key, shape, width, bound, shards=(), dtype=jnp.bfloat16):
    entries = width * jax.random.normal(own_key, shape, jnp.float32)
    if shards:
        entries = entries * levels(own_key, shape, shards, -0.22, 0.18)
    return jnp.clip(entries, -bound, bound).astype(dtype)


def setup_inputs(seed: int = 0) -> dict:
    seeds = jax.random.split(jax.random.key(seed), 5)
    qkv = gaussian(seeds[0], (3, L, C), 1.0, 6.0, ((1, 32), (2, 4)))
    short_weight = gaussian(seeds[1], (3, 3, C), 3 ** -0.5, 3.5, ((2, 4),), jnp.float32)
    long_filter = gaussian(seeds[2], (L, C), (1.0 / (TOK_DEV * N_SEQ) ** 0.5), 0.125, ((0, 32), (1, 4)), jnp.float32)
    skip = gaussian(seeds[3], (C,), 1.0, 4.0, ((0, 4),), jnp.float32)
    return dict(qkv=qkv, short_weight=short_weight, long_filter=long_filter, skip=skip)


def reference(qkv, short_weight, long_filter, skip):
    x = qkv.astype(jnp.float32)
    padded = jnp.pad(x, ((0, 0), (2, 0), (0, 0)))
    z = short_weight[:, 0][:, None, :] * padded[:, 2:] + short_weight[:, 1][:, None, :] * padded[:, 1:-1] + short_weight[:, 2][:, None, :] * padded[:, :-2]
    query = z[0]
    drive = z[1] * z[2]
    block = 128 if C % 128 == 0 else C
    count = C // block
    drive_blocks = drive.reshape(L, count, block).transpose(1, 0, 2)
    filter_blocks = long_filter.reshape(L, count, block).transpose(1, 0, 2)

    def one_block(items):
        signal, kernel = items
        spec = jnp.fft.rfft(signal, n=2 * L, axis=0) * jnp.fft.rfft(kernel, n=2 * L, axis=0)
        return jnp.fft.irfft(spec, n=2 * L, axis=0)[:L].astype(jnp.float32)

    long_blocks = lax.map(one_block, (drive_blocks, filter_blocks))
    long_part = long_blocks.transpose(1, 0, 2).reshape(L, C)
    return (query * (long_part + skip[None, :] * drive)).astype(jnp.bfloat16)
```

```python
import functools

import jax
import jax.numpy as jnp
import numpy as np
from jax import lax
from jax.experimental import pallas as pl
from jax.experimental.pallas import tpu as pltpu
from jax.sharding import PartitionSpec as P

MESH = pl.DeviceIdType.MESH
R = 16
F32 = jnp.float32
BF16 = jnp.bfloat16


def dot(a, b):
    return jnp.dot(a, b, preferred_element_type=F32)


def tables(parts, tok):
    place = np.arange(parts)
    odd = 2 * place + 1
    angle = 2 * np.pi * np.outer(odd, place) / (4 * parts)
    spread = lambda m: np.kron(m, np.eye(R))
    f1 = np.concatenate([spread(np.cos(angle)), spread(-np.sin(angle))], axis=0)
    g1 = np.concatenate([spread(np.cos(angle).T), spread(-np.sin(angle).T)], axis=1)
    offset = np.arange(tok)
    angle = 2 * np.pi * (np.outer(offset, offset) % tok) / tok
    cos, sin = np.cos(angle), np.sin(angle)
    w = np.block([[cos, -sin], [sin, cos]])
    wi = np.block([[cos, sin], [-sin, cos]])
    angle = 2 * np.pi * np.outer(odd, offset) / (4 * parts * tok)
    tw = np.stack([np.cos(angle), np.sin(angle)])
    half = lambda m: jnp.asarray(m.astype(np.float32), BF16)
    return half(f1), half(w), half(wi), half(g1), jnp.asarray(tw.astype(np.float32))


def kernel(
    parts, qkv_hbm, sw_ref, filt_hbm, skip_ref, f1_hbm, w_hbm, wi_hbm, g1_hbm, tw_ref, o_ref,
    qkv, filt, f1, w, wi, g1, halo, ht, dt, hr, xr, ys, lt, drive, query, spec, b, y, g,
    load_sem, halo_sem, send_sem, recv_sem,
):
    me = lax.axis_index("seq")
    ch = lax.axis_index("ch")
    tok = qkv.shape[1]
    chans = qkv.shape[2]
    rows = parts * R
    chunks = chans // rows
    half = tok // 2

    barrier = pltpu.get_barrier_semaphore()

    def greet(k, carry):
        pl.semaphore_signal(barrier, inc=1, device_id=(lax.rem(me + k, parts), ch), device_id_type=MESH)
        return carry

    lax.fori_loop(1, parts, greet, 0)

    loads = [
        pltpu.make_async_copy(src, dst, load_sem.at[i])
        for i, (src, dst) in enumerate(
            [(filt_hbm, filt), (qkv_hbm, qkv), (f1_hbm, f1), (w_hbm, w), (wi_hbm, wi), (g1_hbm, g1)]
        )
    ]
    for load in loads:
        load.start()

    loads[0].wait()

    def turn_filter(j, carry):
        at = pl.ds(pl.multiple_of(j * 128, 128), 128)
        ht[at, :] = filt[:, at].T.astype(BF16)
        return carry

    lax.fori_loop(0, chans // 128, turn_filter, 0)
    loads[1].wait()
    pl.semaphore_wait(barrier, parts - 1)

    edge = pltpu.make_async_remote_copy(
        src_ref=qkv.at[:, pl.ds(tok - 16, 16), :], dst_ref=halo, send_sem=halo_sem.at[0], recv_sem=halo_sem.at[1],
        device_id=(lax.rem(me + 1, parts), ch), device_id_type=MESH,
    )
    edge.start()

    def deal(kind, chunk, src, dst):
        base = chunk * rows

        def one(k, carry):
            to = lax.rem(me + k, parts)
            pltpu.make_async_remote_copy(
                src_ref=src.at[pl.ds(pl.multiple_of(base + to * R, R), R), :],
                dst_ref=dst.at[pl.ds(pl.multiple_of(base + me * R, R), R), :],
                send_sem=send_sem.at[kind, chunk],
                recv_sem=recv_sem.at[kind, chunk],
                device_id=(to, ch),
                device_id_type=MESH,
            ).start()
            return carry

        lax.fori_loop(1, parts, one, 0)
        own = pl.ds(pl.multiple_of(base + me * R, R), R)
        pltpu.make_async_copy(src.at[own, :], dst.at[own, :], recv_sem.at[kind, chunk]).start()

    def arrived(kind, chunk, dst):
        whole = dst.at[pl.ds(chunk * rows, rows), :]
        pltpu.make_async_copy(whole, whole, recv_sem.at[kind, chunk]).wait()

    def left(kind, chunk, src):
        sent = src.at[pl.ds(0, rows - R), :]
        pltpu.make_async_copy(sent, sent, send_sem.at[kind, chunk]).wait()

    for chunk in range(chunks):
        deal(0, chunk, ht, hr)

    edge.wait_recv()
    first = jnp.where(me > 0, 1.0, 0.0).astype(F32)

    def short(m, at):
        before = halo[m, :, at].astype(F32)[8:, :] * first
        ext = jnp.concatenate([before, qkv[m, :, at].astype(F32)], axis=0)
        return (
            sw_ref[m, 0:1, at] * ext[8:, :]
            + sw_ref[m, 1:2, at] * ext[7:-1, :]
            + sw_ref[m, 2:3, at] * ext[6:-2, :]
        )

    for chunk in range(chunks):

        def gate(j, carry):
            at = pl.ds(pl.multiple_of(chunk * rows + j * 128, 128), 128)
            value = short(1, at) * short(2, at)
            drive[:, at] = value
            dt[at, :] = value.T.astype(BF16)
            return carry

        lax.fori_loop(0, rows // 128, gate, 0)
        deal(1, chunk, dt, xr)

    def ask(j, carry):
        at = pl.ds(pl.multiple_of(j * 128, 128), 128)
        query[:, at] = short(0, at)
        return carry

    lax.fori_loop(0, chans // 128, ask, 0)

    def along_parts(blocks, chunk):
        for j in range(2):
            real = dot(f1[j * rows // 2 : (j + 1) * rows // 2, :], blocks)
            imag = dot(f1[rows + j * rows // 2 : rows + (j + 1) * rows // 2, :], blocks)
            for k in range(parts // 2):
                at = j * (parts // 2) + k
                cos, sin = tw_ref[0, at : at + 1, :], tw_ref[1, at : at + 1, :]
                re, im = real[k * R : (k + 1) * R, :], imag[k * R : (k + 1) * R, :]
                b[at * R : (at + 1) * R, :tok] = (re * cos + im * sin).astype(BF16)
                b[at * R : (at + 1) * R, tok:] = (im * cos - re * sin).astype(BF16)

    for load in loads[2:]:
        load.wait()

    for chunk in range(chunks):
        arrived(0, chunk, hr)
        along_parts(hr[pl.ds(chunk * rows, rows), :], chunk)
        for n in range(4):
            spec[chunk, :, n * half : (n + 1) * half] = dot(b[...], w[:, n * half : (n + 1) * half])

    for chunk in range(chunks):
        arrived(1, chunk, xr)
        along_parts(xr[pl.ds(chunk * rows, rows), :], chunk)
        for n in range(2):
            real_at, imag_at = slice(n * half, (n + 1) * half), slice(tok + n * half, tok + (n + 1) * half)
            xre, xim = dot(b[...], w[:, real_at]), dot(b[...], w[:, imag_at])
            hre, him = spec[chunk, :, real_at], spec[chunk, :, imag_at]
            y[:, real_at] = (xre * hre - xim * him).astype(BF16)
            y[:, imag_at] = (xre * him + xim * hre).astype(BF16)
        for n in range(2):
            real_at, imag_at = slice(n * half, (n + 1) * half), slice(tok + n * half, tok + (n + 1) * half)
            gre, gim = dot(y[...], wi[:, real_at]), dot(y[...], wi[:, imag_at])
            for k in range(parts):
                scale = 2.0 / (2 * parts * tok)
                cos, sin = tw_ref[0, k : k + 1, real_at] * scale, tw_ref[1, k : k + 1, real_at] * scale
                re, im = gre[k * R : (k + 1) * R, :], gim[k * R : (k + 1) * R, :]
                g[k * R : (k + 1) * R, real_at] = (re * cos - im * sin).astype(BF16)
                g[rows + k * R : rows + (k + 1) * R, real_at] = (im * cos + re * sin).astype(BF16)
        for n in range(2):
            at = slice(n * half, (n + 1) * half)
            ys[pl.ds(chunk * rows, rows), at] = dot(g1[...], g[:, at]).astype(BF16)
        deal(2, chunk, ys, lt)

    for chunk in range(chunks):
        arrived(2, chunk, lt)

        def finish(j, carry):
            at = pl.ds(pl.multiple_of(chunk * rows + j * 128, 128), 128)
            long_part = lt[at, :].astype(F32).T
            o_ref[:, at] = (query[:, at] * (long_part + skip_ref[0:1, at] * drive[:, at])).astype(BF16)
            return carry

        lax.fori_loop(0, rows // 128, finish, 0)

    edge.wait_send()
    for chunk in range(chunks):
        left(0, chunk, ht)
        left(1, chunk, dt)
        left(2, chunk, ys)


def solution(mesh):
    parts = mesh.shape["seq"]

    def on_device(qkv, short_weight, long_filter, skip):
        tok, chans = long_filter.shape
        rows = parts * R
        chunks = chans // rows
        f1, w, wi, g1, tw = tables(parts, tok)
        vmem = pl.BlockSpec(memory_space=pltpu.VMEM)
        hbm = pl.BlockSpec(memory_space=pl.ANY)
        return pl.pallas_call(
            functools.partial(kernel, parts),
            out_shape=jax.ShapeDtypeStruct((tok, chans), BF16),
            in_specs=[hbm, vmem, hbm, vmem, hbm, hbm, hbm, hbm, vmem],
            out_specs=vmem,
            scratch_shapes=[
                pltpu.VMEM(qkv.shape, BF16),
                pltpu.VMEM((tok, chans), F32),
                pltpu.VMEM(f1.shape, BF16),
                pltpu.VMEM(w.shape, BF16),
                pltpu.VMEM(wi.shape, BF16),
                pltpu.VMEM(g1.shape, BF16),
                pltpu.VMEM((3, 16, chans), BF16),
                pltpu.VMEM((chans, tok), BF16),
                pltpu.VMEM((chans, tok), BF16),
                pltpu.VMEM((chans, tok), BF16),
                pltpu.VMEM((chans, tok), BF16),
                pltpu.VMEM((chans, tok), BF16),
                pltpu.VMEM((chans, tok), BF16),
                pltpu.VMEM((tok, chans), F32),
                pltpu.VMEM((tok, chans), F32),
                pltpu.VMEM((chunks, rows, 2 * tok), F32),
                pltpu.VMEM((rows, 2 * tok), BF16),
                pltpu.VMEM((rows, 2 * tok), BF16),
                pltpu.VMEM((2 * rows, tok), BF16),
                pltpu.SemaphoreType.DMA((6,)),
                pltpu.SemaphoreType.DMA((2,)),
                pltpu.SemaphoreType.DMA((3, chunks)),
                pltpu.SemaphoreType.DMA((3, chunks)),
            ],
            compiler_params=pltpu.CompilerParams(
                collective_id=0, has_side_effects=True, vmem_limit_bytes=60 * 2**20
            ),
        )(qkv, short_weight, long_filter, skip[None, :], f1, w, wi, g1, tw)

    return jax.shard_map(
        on_device,
        mesh=mesh,
        in_specs=(P(None, "seq", "ch"), P(None, None, "ch"), P("seq", "ch"), P("ch")),
        out_specs=P("seq", "ch"),
        check_vma=False,
    )
```

```python
import functools

import jax
import jax.numpy as jnp
import numpy as np
from jax import lax
from jax.experimental import pallas as pl
from jax.experimental.pallas import tpu as pltpu
from jax.sharding import PartitionSpec as P

MESH = pl.DeviceIdType.MESH
R = 16
STEPS = ((2, 2), (2, 1), (1, 2), (2, 3), (3, 2), (1, 1), (3, 3), (1, 3), (3, 1), (2, 0), (0, 2), (0, 1), (1, 0), (0, 3), (3, 0))
F32 = jnp.float32
BF16 = jnp.bfloat16


def dot(a, b):
    return jnp.dot(a, b, preferred_element_type=F32)


def tables(parts, tok):
    place = np.arange(parts)
    odd = 2 * place + 1
    angle = 2 * np.pi * np.outer(odd, place) / (4 * parts)
    spread = lambda m: np.kron(m, np.eye(R))
    f1 = np.concatenate([spread(np.cos(angle)), spread(-np.sin(angle))], axis=0)
    g1 = np.concatenate([spread(np.cos(angle).T), spread(-np.sin(angle).T)], axis=1)
    offset = np.arange(tok)
    angle = 2 * np.pi * (np.outer(offset, offset) % tok) / tok
    cos, sin = np.cos(angle), np.sin(angle)
    w = np.block([[cos, -sin], [sin, cos]])
    wi = np.block([[cos, sin], [-sin, cos]])
    angle = 2 * np.pi * np.outer(odd, offset) / (4 * parts * tok)
    tw = np.stack([np.cos(angle), np.sin(angle)])
    half = lambda m: jnp.asarray(m.astype(np.float32), BF16)
    return half(f1), half(w), half(wi), half(g1), jnp.asarray(tw.astype(np.float32))


def kernel(
    parts, qkv_hbm, sw_ref, filt_hbm, skip_ref, f1_hbm, w_hbm, wi_hbm, g1_hbm, tw_ref, o_ref,
    qkv, filt, f1, w, wi, g1, tail, ends, halo, ht, dt, hr, xr, ys, lt, drive, query, spec, b, y, g,
    load_sem, halo_sem, send_sem, recv_sem,
):
    me = lax.axis_index("seq")
    ch = lax.axis_index("ch")
    tok = qkv.shape[1]
    chans = qkv.shape[2]
    rows = parts * R
    chunks = chans // rows
    half = tok // 2

    lanes = [pl.ds(chunk * rows, rows) for chunk in range(chunks)]
    loads = [
        pltpu.make_async_copy(src, dst, load_sem.at[i])
        for i, (src, dst) in enumerate(
            [(filt_hbm.at[:, at], filt.at[:, at]) for at in lanes]
            + [(qkv_hbm.at[:, pl.ds(tok - 16, 16), :], tail)]
            + [(qkv_hbm, qkv), (f1_hbm, f1), (w_hbm, w), (wi_hbm, wi), (g1_hbm, g1)]
        )
    ]
    for load in loads[: chunks + 1]:
        load.start()

    barrier = pltpu.get_barrier_semaphore()

    def greet(k, carry):
        pl.semaphore_signal(barrier, inc=1, device_id=((me + k) & (parts - 1), ch), device_id_type=MESH)
        return carry

    lax.fori_loop(1, parts, greet, 0)

    def turn_filter(j, carry):
        at = pl.ds(pl.multiple_of(j * 128, 128), 128)
        ht[at, :] = filt[:, at].T.astype(BF16)
        return carry

    loads[0].wait()
    lax.fori_loop(0, rows // 128, turn_filter, 0)
    loads[chunks].wait()
    last = [tail[m].astype(F32)[14:, :] for m in range(3)]
    ends[...] = jnp.concatenate(last + [jnp.zeros((10, chans), F32)], axis=0).astype(BF16)
    pl.semaphore_wait(barrier, parts - 1)

    edge = pltpu.make_async_remote_copy(
        src_ref=ends, dst_ref=halo, send_sem=halo_sem.at[0], recv_sem=halo_sem.at[1],
        device_id=((me + 1) & (parts - 1), ch), device_id_type=MESH,
    )
    edge.start()

    def deal(kind, chunk, src, dst):
        base = chunk * rows

        def send(to):
            pltpu.make_async_remote_copy(
                src_ref=src.at[pl.ds(pl.multiple_of(base + to * R, R), R), :],
                dst_ref=dst.at[pl.ds(pl.multiple_of(base + me * R, R), R), :],
                send_sem=send_sem.at[kind, chunk],
                recv_sem=recv_sem.at[kind, chunk],
                device_id=(to, ch),
                device_id_type=MESH,
            ).start()

        z, x, core = me >> 3, (me >> 1) & 3, me & 1
        for flip in range(2):
            for steps in (STEPS[:8], STEPS[8:]):
                code = sum((4 * dz + dx) << (4 * i) for i, (dz, dx) in enumerate(steps))
                code = code - 2**32 if code >= 2**31 else code

                def one(k, carry):
                    step = (jnp.int32(code) >> (4 * k)) & 15
                    send((((z + (step >> 2)) & 3) << 3) + (((x + step) & 3) << 1) + (core ^ flip))
                    return carry

                lax.fori_loop(0, len(steps), one, 0)
        send(me ^ 1)
        own = pl.ds(pl.multiple_of(base + me * R, R), R)
        pltpu.make_async_copy(src.at[own, :], dst.at[own, :], recv_sem.at[kind, chunk]).start()

    def arrived(kind, chunk, dst):
        whole = dst.at[pl.ds(chunk * rows, rows), :]
        pltpu.make_async_copy(whole, whole, recv_sem.at[kind, chunk]).wait()

    def left(kind, chunk, src):
        sent = src.at[pl.ds(0, rows - R), :]
        pltpu.make_async_copy(sent, sent, send_sem.at[kind, chunk]).wait()

    deal(0, 0, ht, hr)
    for load in loads[chunks + 1 :]:
        load.start()
    for chunk in range(1, chunks):
        loads[chunk].wait()
        lax.fori_loop(chunk * rows // 128, (chunk + 1) * rows // 128, turn_filter, 0)
        deal(0, chunk, ht, hr)

    loads[chunks + 1].wait()
    edge.wait_recv()
    first = jnp.where(me > 0, 1.0, 0.0).astype(F32)

    def short(m, at):
        before = halo[:, at].astype(F32)[2 * m : 2 * m + 2, :] * first
        before = jnp.concatenate([jnp.zeros((6, 128), F32), before], axis=0)
        ext = jnp.concatenate([before, qkv[m, :, at].astype(F32)], axis=0)
        return (
            sw_ref[m, 0:1, at] * ext[8:, :]
            + sw_ref[m, 1:2, at] * ext[7:-1, :]
            + sw_ref[m, 2:3, at] * ext[6:-2, :]
        )

    for chunk in range(chunks):

        def gate(j, carry):
            at = pl.ds(pl.multiple_of(chunk * rows + j * 128, 128), 128)
            value = short(1, at) * short(2, at)
            drive[:, at] = value
            dt[at, :] = value.T.astype(BF16)
            return carry

        lax.fori_loop(0, rows // 128, gate, 0)
        deal(1, chunk, dt, xr)

    def ask(j, carry):
        at = pl.ds(pl.multiple_of(j * 128, 128), 128)
        query[:, at] = short(0, at)
        return carry

    lax.fori_loop(0, chans // 128, ask, 0)

    def along_parts(blocks, chunk):
        for j in range(2):
            real = dot(f1[j * rows // 2 : (j + 1) * rows // 2, :], blocks)
            imag = dot(f1[rows + j * rows // 2 : rows + (j + 1) * rows // 2, :], blocks)
            for k in range(parts // 2):
                at = j * (parts // 2) + k
                cos, sin = tw_ref[0, at : at + 1, :], tw_ref[1, at : at + 1, :]
                re, im = real[k * R : (k + 1) * R, :], imag[k * R : (k + 1) * R, :]
                b[at * R : (at + 1) * R, :tok] = (re * cos + im * sin).astype(BF16)
                b[at * R : (at + 1) * R, tok:] = (im * cos - re * sin).astype(BF16)

    for load in loads[chunks + 2 :]:
        load.wait()

    for chunk in range(chunks):
        arrived(0, chunk, hr)
        along_parts(hr[pl.ds(chunk * rows, rows), :], chunk)
        for n in range(4):
            spec[chunk, :, n * half : (n + 1) * half] = dot(b[...], w[:, n * half : (n + 1) * half])

    for chunk in range(chunks):
        arrived(1, chunk, xr)
        along_parts(xr[pl.ds(chunk * rows, rows), :], chunk)
        for n in range(2):
            real_at, imag_at = slice(n * half, (n + 1) * half), slice(tok + n * half, tok + (n + 1) * half)
            xre, xim = dot(b[...], w[:, real_at]), dot(b[...], w[:, imag_at])
            hre, him = spec[chunk, :, real_at], spec[chunk, :, imag_at]
            y[:, real_at] = (xre * hre - xim * him).astype(BF16)
            y[:, imag_at] = (xre * him + xim * hre).astype(BF16)
        for n in range(2):
            real_at, imag_at = slice(n * half, (n + 1) * half), slice(tok + n * half, tok + (n + 1) * half)
            gre, gim = dot(y[...], wi[:, real_at]), dot(y[...], wi[:, imag_at])
            for k in range(parts):
                scale = 2.0 / (2 * parts * tok)
                cos, sin = tw_ref[0, k : k + 1, real_at] * scale, tw_ref[1, k : k + 1, real_at] * scale
                re, im = gre[k * R : (k + 1) * R, :], gim[k * R : (k + 1) * R, :]
                g[k * R : (k + 1) * R, real_at] = (re * cos - im * sin).astype(BF16)
                g[rows + k * R : rows + (k + 1) * R, real_at] = (im * cos + re * sin).astype(BF16)
        for n in range(2):
            at = slice(n * half, (n + 1) * half)
            ys[pl.ds(chunk * rows, rows), at] = dot(g1[...], g[:, at]).astype(BF16)
        deal(2, chunk, ys, lt)

    for chunk in range(chunks):
        arrived(2, chunk, lt)

        def finish(j, carry):
            at = pl.ds(pl.multiple_of(chunk * rows + j * 128, 128), 128)
            long_part = lt[at, :].astype(F32).T
            o_ref[:, at] = (query[:, at] * (long_part + skip_ref[0:1, at] * drive[:, at])).astype(BF16)
            return carry

        lax.fori_loop(0, rows // 128, finish, 0)

    edge.wait_send()
    for chunk in range(chunks):
        left(0, chunk, ht)
        left(1, chunk, dt)
        left(2, chunk, ys)


def solution(mesh):
    parts = mesh.shape["seq"]

    def on_device(qkv, short_weight, long_filter, skip):
        tok, chans = long_filter.shape
        rows = parts * R
        chunks = chans // rows
        f1, w, wi, g1, tw = tables(parts, tok)
        vmem = pl.BlockSpec(memory_space=pltpu.VMEM)
        hbm = pl.BlockSpec(memory_space=pl.ANY)
        return pl.pallas_call(
            functools.partial(kernel, parts),
            out_shape=pltpu.VMEM((tok, chans), BF16),
            in_specs=[hbm, vmem, hbm, vmem, hbm, hbm, hbm, hbm, vmem],
            out_specs=vmem,
            scratch_shapes=[
                pltpu.VMEM(qkv.shape, BF16),
                pltpu.VMEM((tok, chans), F32),
                pltpu.VMEM(f1.shape, BF16),
                pltpu.VMEM(w.shape, BF16),
                pltpu.VMEM(wi.shape, BF16),
                pltpu.VMEM(g1.shape, BF16),
                pltpu.VMEM((3, 16, chans), BF16),
                pltpu.VMEM((16, chans), BF16),
                pltpu.VMEM((16, chans), BF16),
                pltpu.VMEM((chans, tok), BF16),
                pltpu.VMEM((chans, tok), BF16),
                pltpu.VMEM((chans, tok), BF16),
                pltpu.VMEM((chans, tok), BF16),
                pltpu.VMEM((chans, tok), BF16),
                pltpu.VMEM((chans, tok), BF16),
                pltpu.VMEM((tok, chans), F32),
                pltpu.VMEM((tok, chans), F32),
                pltpu.VMEM((chunks, rows, 2 * tok), F32),
                pltpu.VMEM((rows, 2 * tok), BF16),
                pltpu.VMEM((rows, 2 * tok), BF16),
                pltpu.VMEM((2 * rows, tok), BF16),
                pltpu.SemaphoreType.DMA((chunks + 6,)),
                pltpu.SemaphoreType.DMA((2,)),
                pltpu.SemaphoreType.DMA((3, chunks)),
                pltpu.SemaphoreType.DMA((3, chunks)),
            ],
            compiler_params=pltpu.CompilerParams(
                collective_id=0, has_side_effects=True, vmem_limit_bytes=60 * 2**20
            ),
        )(qkv, short_weight, long_filter, skip[None, :], f1, w, wi, g1, tw)

    return jax.shard_map(
        on_device,
        mesh=mesh,
        in_specs=(P(None, "seq", "ch"), P(None, None, "ch"), P("seq", "ch"), P("ch")),
        out_specs=P("seq", "ch"),
        check_vma=False,
    )
```

```python
import functools

import jax
import jax.numpy as jnp
import numpy as np
from jax import lax
from jax.experimental import pallas as pl
from jax.experimental.pallas import tpu as pltpu
from jax.sharding import PartitionSpec as P

MESH = pl.DeviceIdType.MESH
C = 8
R = 16
STEPS = ((2, 2), (2, 1), (1, 2), (2, 3), (3, 2), (1, 1), (3, 3), (1, 3), (3, 1), (2, 0), (0, 2), (0, 1), (1, 0), (0, 3), (3, 0))
F32 = jnp.float32
BF16 = jnp.bfloat16


def dot(a, b):
    return jnp.dot(a, b, preferred_element_type=F32)


def tables(parts, tok):
    place = np.arange(parts)
    odd = 2 * place + 1
    angle = 2 * np.pi * np.outer(odd, place) / (4 * parts)
    spread = lambda m: np.kron(m, np.eye(R))
    f1 = np.concatenate([spread(np.cos(angle)), spread(-np.sin(angle))], axis=0)
    g1 = np.concatenate([spread(np.cos(angle).T), spread(-np.sin(angle).T)], axis=1)
    offset = np.arange(tok)
    angle = 2 * np.pi * (np.outer(offset, offset) % tok) / tok
    cos, sin = np.cos(angle), np.sin(angle)
    w = np.block([[cos, -sin], [sin, cos]])
    wi = np.block([[cos, sin], [-sin, cos]])
    angle = 2 * np.pi * np.outer(odd, offset) / (4 * parts * tok)
    tw = np.stack([np.cos(angle), np.sin(angle)])
    half = lambda m: m.astype(np.float32).astype(BF16)
    rest = lambda m: half(m - half(m).astype(np.float64))
    f1 = np.stack([half(f1), rest(f1)])
    g1 = np.stack([half(g1), rest(g1)])
    return f1, half(w), half(wi), g1, tw.astype(np.float32)


def kernel(
    parts, qkv_hbm, sw_hbm, filt_hbm, skip_hbm, f1_hbm, w_hbm, wi_hbm, g1_hbm, tw_hbm, o_ref,
    sw_ref, skip_ref, tw_ref, qkv, filt, f1, w, wi, g1, tail, ends, halo, ht, dt, hr, xr, ys, lt, drive, query, spec, b, y, g,
    load_sem, halo_sem, send_sem, recv_sem,
):
    me = lax.axis_index("seq")
    ch = lax.axis_index("ch")
    tok = qkv.shape[1]
    chans = qkv.shape[2]
    rows = parts * R
    lines = parts * C
    chunks = chans // lines
    half = tok // 2

    lanes = [pl.ds(chunk * lines, lines) for chunk in range(chunks)]
    loads = [
        pltpu.make_async_copy(src, dst, load_sem.at[i])
        for i, (src, dst) in enumerate(
            [(filt_hbm.at[:, at], filt.at[:, at]) for at in lanes]
            + [(qkv_hbm.at[:, pl.ds(tok - 16, 16), :], tail)]
            + [(qkv_hbm, qkv), (sw_hbm, sw_ref), (skip_hbm, skip_ref), (tw_hbm, tw_ref), (f1_hbm, f1), (w_hbm, w), (wi_hbm, wi), (g1_hbm, g1)]
        )
    ]
    for load in loads[: chunks + 1]:
        load.start()

    barrier = pltpu.get_barrier_semaphore()

    z, x, core = me >> 3, (me >> 1) & 3, me & 1

    def tour(steps, visit):
        for flip in range(2):
            for some in (steps[:8], steps[8:]):
                code = sum((4 * dz + dx) << (4 * i) for i, (dz, dx) in enumerate(some))
                code = code - 2**32 if code >= 2**31 else code

                def one(k, carry):
                    step = (jnp.int32(code) >> (4 * k)) & 15
                    visit((((z + (step >> 2)) & 3) << 3) + (((x + step) & 3) << 1) + (core ^ flip))
                    return carry

                lax.fori_loop(0, len(some), one, 0)
        visit(me ^ 1)

    def greet(to):
        pl.semaphore_signal(barrier, inc=1, device_id=(to, ch), device_id_type=MESH)

    tour(STEPS, greet)

    def turn(dst, j, value):
        value = value.T
        for d in range(128 // C):
            mine = value[d * C : (d + 1) * C, :]
            message = jnp.concatenate([mine[:, :half], mine[:, half:]], axis=0).astype(BF16)
            dst[pl.ds(pl.multiple_of(j * 128 * R // C + d * R, R), R), :] = message

    def turn_filter(j, carry):
        turn(ht, j, filt[:, pl.ds(pl.multiple_of(j * 128, 128), 128)])
        return carry

    loads[0].wait()
    lax.fori_loop(0, lines // 128, turn_filter, 0)
    loads[chunks].wait()
    last = [tail[m].astype(F32)[14:, :] for m in range(3)]
    ends[...] = jnp.concatenate(last + [jnp.zeros((10, chans), F32)], axis=0).astype(BF16)
    pl.semaphore_wait(barrier, parts - 1)

    edge = pltpu.make_async_remote_copy(
        src_ref=ends, dst_ref=halo, send_sem=halo_sem.at[0], recv_sem=halo_sem.at[1],
        device_id=((me + 1) & (parts - 1), ch), device_id_type=MESH,
    )
    edge.start()

    def deal(kind, chunk, src, dst):
        base = chunk * rows

        def send(to):
            pltpu.make_async_remote_copy(
                src_ref=src.at[pl.ds(pl.multiple_of(base + to * R, R), R), :],
                dst_ref=dst.at[pl.ds(pl.multiple_of(base + me * R, R), R), :],
                send_sem=send_sem.at[kind, chunk],
                recv_sem=recv_sem.at[kind, chunk],
                device_id=(to, ch),
                device_id_type=MESH,
            ).start()

        tour(STEPS, send)
        own = pl.ds(pl.multiple_of(base + me * R, R), R)
        pltpu.make_async_copy(src.at[own, :], dst.at[own, :], recv_sem.at[kind, chunk]).start()

    def arrived(kind, chunk, dst):
        whole = dst.at[pl.ds(pl.multiple_of(chunk * rows, rows), rows), :]
        pltpu.make_async_copy(whole, whole, recv_sem.at[kind, chunk]).wait()

    def left(kind, chunk, src):
        sent = src.at[pl.ds(0, rows - R), :]
        pltpu.make_async_copy(sent, sent, send_sem.at[kind, chunk]).wait()

    deal(0, 0, ht, hr)
    for load in loads[chunks + 1 :]:
        load.start()
    loads[chunks + 1].wait()
    loads[chunks + 2].wait()
    edge.wait_recv()
    first = jnp.where(me > 0, 1.0, 0.0).astype(F32)

    def short(m, at):
        before = halo[:, at].astype(F32)[2 * m : 2 * m + 2, :] * first
        before = jnp.concatenate([jnp.zeros((6, 128), F32), before], axis=0)
        ext = jnp.concatenate([before, qkv[m, :, at].astype(F32)], axis=0)
        return (
            sw_ref[m, 0:1, at] * ext[8:, :]
            + sw_ref[m, 1:2, at] * ext[7:-1, :]
            + sw_ref[m, 2:3, at] * ext[6:-2, :]
        )

    for chunk in range(chunks):

        def gate(j, carry):
            at = pl.ds(pl.multiple_of(j * 128, 128), 128)
            value = short(1, at) * short(2, at)
            drive[:, at] = value
            turn(dt, j, value)
            return carry

        if chunk:
            loads[chunk].wait()
            lax.fori_loop(chunk * lines // 128, (chunk + 1) * lines // 128, turn_filter, 0)
            deal(0, chunk, ht, hr)
        lax.fori_loop(chunk * lines // 128, (chunk + 1) * lines // 128, gate, 0)
        deal(1, chunk, dt, xr)

    def ask(j, carry):
        at = pl.ds(pl.multiple_of(j * 128, 128), 128)
        query[:, at] = short(0, at)
        return carry

    lax.fori_loop(0, chans // 128, ask, 0)

    def split(m_ref, at, value):
        return dot(m_ref[0, at, :], value) + dot(m_ref[1, at, :], value)

    def along_parts(blocks):
        real, imag = split(f1, slice(0, rows), blocks), split(f1, slice(rows, 2 * rows), blocks)
        for k in range(0, parts, 2):
            for n in range(2):
                at = slice(n * half, (n + 1) * half)
                turned = []
                for p in (k, k + 1):
                    cos, sin = tw_ref[0, p : p + 1, at], tw_ref[1, p : p + 1, at]
                    here = slice(p * R + n * C, p * R + (n + 1) * C)
                    re, im = real[here, :], imag[here, :]
                    turned.append((re * cos + im * sin, im * cos - re * sin))
                b[k * C : (k + 2) * C, n * half : (n + 1) * half] = jnp.concatenate(
                    [t[0] for t in turned], axis=0
                ).astype(BF16)
                b[k * C : (k + 2) * C, tok + n * half : tok + (n + 1) * half] = jnp.concatenate(
                    [t[1] for t in turned], axis=0
                ).astype(BF16)

    for load in loads[chunks + 3 :]:
        load.wait()

    def place(chunk):
        return pl.ds(pl.multiple_of(chunk * rows, rows), rows)

    def filter_spectra(chunk):
        arrived(0, chunk, hr)
        along_parts(hr[place(chunk), :])
        for n in range(4):
            spec[:, n * half : (n + 1) * half] = dot(b[...], w[:, n * half : (n + 1) * half])

    def convolve(chunk):
        arrived(1, chunk, xr)
        along_parts(xr[place(chunk), :])
        for n in range(2):
            real_at, imag_at = slice(n * half, (n + 1) * half), slice(tok + n * half, tok + (n + 1) * half)
            xre, xim = dot(b[...], w[:, real_at]), dot(b[...], w[:, imag_at])
            hre, him = spec[:, real_at], spec[:, imag_at]
            y[:, real_at] = (xre * hre - xim * him).astype(BF16)
            y[:, imag_at] = (xre * him + xim * hre).astype(BF16)
        back = [dot(y[...], wi[:, n * half : (n + 1) * half]) for n in range(4)]
        scale = 2.0 / (2 * parts * tok)
        for k in range(parts):
            turned = []
            for n in range(2):
                at = slice(n * half, (n + 1) * half)
                cos, sin = tw_ref[0, k : k + 1, at] * scale, tw_ref[1, k : k + 1, at] * scale
                re, im = back[n][k * C : (k + 1) * C, :], back[2 + n][k * C : (k + 1) * C, :]
                turned.append((re * cos - im * sin, im * cos + re * sin))
            for part in range(2):
                g[part * rows + k * R : part * rows + (k + 1) * R, :] = jnp.concatenate(
                    [t[part] for t in turned], axis=0
                ).astype(BF16)
        ys[place(chunk), :] = split(g1, slice(0, rows), g[...]).astype(BF16)

    def one_chunk(chunk, carry):
        filter_spectra(chunk)
        convolve(chunk)
        deal(2, chunk, ys, lt)
        return carry

    lax.fori_loop(0, chunks, one_chunk, 0)

    def finish(j, carry):
        at = pl.ds(pl.multiple_of(j * 128, 128), 128)
        came = lt[pl.ds(pl.multiple_of(j * 128 * R // C, 128 * R // C), 128 * R // C), :].astype(F32)
        for n in range(2):
            long_part = jnp.concatenate(
                [came[d * R + n * C : d * R + (n + 1) * C, :] for d in range(128 // C)], axis=0
            ).T
            here = slice(n * half, (n + 1) * half)
            o_ref[here, at] = (
                query[here, at] * (long_part + skip_ref[0:1, at] * drive[here, at])
            ).astype(BF16)
        return carry

    for chunk in range(chunks):
        arrived(2, chunk, lt)
        lax.fori_loop(chunk * lines // 128, (chunk + 1) * lines // 128, finish, 0)

    edge.wait_send()
    for chunk in range(chunks):
        left(0, chunk, ht)
        left(1, chunk, dt)
        left(2, chunk, ys)


def solution(mesh):
    parts = mesh.shape["seq"]

    def on_device(qkv, short_weight, long_filter, skip):
        tok, chans = long_filter.shape
        rows, lines = parts * R, parts * C
        chunks = chans // lines
        f1, w, wi, g1, tw = tables(parts, tok)
        vmem = pl.BlockSpec(memory_space=pltpu.VMEM)
        hbm = pl.BlockSpec(memory_space=pl.ANY)
        return pl.pallas_call(
            functools.partial(kernel, parts),
            out_shape=pltpu.VMEM((tok, chans), BF16),
            in_specs=[hbm] * 9,
            out_specs=vmem,
            scratch_shapes=[
                pltpu.VMEM(short_weight.shape, F32),
                pltpu.VMEM((1, chans), F32),
                pltpu.VMEM(tw.shape, F32),
                pltpu.VMEM(qkv.shape, BF16),
                pltpu.VMEM((tok, chans), F32),
                pltpu.VMEM(f1.shape, BF16),
                pltpu.VMEM(w.shape, BF16),
                pltpu.VMEM(wi.shape, BF16),
                pltpu.VMEM(g1.shape, BF16),
                pltpu.VMEM((3, 16, chans), BF16),
                pltpu.VMEM((16, chans), BF16),
                pltpu.VMEM((16, chans), BF16),
                pltpu.VMEM((chunks * rows, tok // 2), BF16),
                pltpu.VMEM((chunks * rows, tok // 2), BF16),
                pltpu.VMEM((chunks * rows, tok // 2), BF16),
                pltpu.VMEM((chunks * rows, tok // 2), BF16),
                pltpu.VMEM((chunks * rows, tok // 2), BF16),
                pltpu.VMEM((chunks * rows, tok // 2), BF16),
                pltpu.VMEM((tok, chans), F32),
                pltpu.VMEM((tok, chans), F32),
                pltpu.VMEM((lines, 2 * tok), F32),
                pltpu.VMEM((lines, 2 * tok), BF16),
                pltpu.VMEM((lines, 2 * tok), BF16),
                pltpu.VMEM((2 * rows, tok // 2), BF16),
                pltpu.SemaphoreType.DMA((chunks + 9,)),
                pltpu.SemaphoreType.DMA((2,)),
                pltpu.SemaphoreType.DMA((3, chunks)),
                pltpu.SemaphoreType.DMA((3, chunks)),
            ],
            compiler_params=pltpu.CompilerParams(
                collective_id=0, has_side_effects=True, vmem_limit_bytes=60 * 2**20
            ),
        )(qkv, short_weight, long_filter, skip[None, :], f1, w, wi, g1, tw)

    return jax.shard_map(
        on_device,
        mesh=mesh,
        in_specs=(P(None, "seq", "ch"), P(None, None, "ch"), P("seq", "ch"), P("ch")),
        out_specs=P("seq", "ch"),
        check_vma=False,
    )
```

```python
import functools

import jax
import jax.numpy as jnp
import numpy as np
from jax import lax
from jax.experimental import pallas as pl
from jax.experimental.pallas import tpu as pltpu
from jax.sharding import PartitionSpec as P

MESH = pl.DeviceIdType.MESH
C = 8
R = 16
STEPS = ((2, 2), (2, 1), (1, 2), (2, 3), (3, 2), (1, 1), (3, 3), (1, 3), (3, 1), (2, 0), (0, 2), (0, 1), (1, 0), (0, 3), (3, 0))
F32 = jnp.float32
BF16 = jnp.bfloat16


def dot(a, b):
    return jnp.dot(a, b, preferred_element_type=F32)


def tables(parts, tok):
    place = np.arange(parts)
    odd = 2 * place + 1
    angle = 2 * np.pi * np.outer(odd, place) / (4 * parts)
    spread = lambda m: np.kron(m, np.eye(R))
    f1 = np.concatenate([spread(np.cos(angle)), spread(-np.sin(angle))], axis=0)
    g1 = np.concatenate([spread(np.cos(angle).T), spread(-np.sin(angle).T)], axis=1)
    offset = np.arange(tok)
    angle = 2 * np.pi * (np.outer(offset, offset) % tok) / tok
    cos, sin = np.cos(angle), np.sin(angle)
    w = np.block([[cos, -sin], [sin, cos]])
    wi = np.block([[cos, sin], [-sin, cos]])
    angle = 2 * np.pi * np.outer(odd, offset) / (4 * parts * tok)
    tw = np.stack([np.cos(angle), np.sin(angle)])
    half = lambda m: m.astype(np.float32).astype(BF16)
    rest = lambda m: half(m - half(m).astype(np.float64))
    f1 = np.stack([half(f1), rest(f1)])
    g1 = np.stack([half(g1), rest(g1)])
    return f1, half(w), half(wi), g1, tw.astype(np.float32)


def kernel(
    parts, qkv_hbm, sw_hbm, filt_hbm, skip_hbm, f1_hbm, w_hbm, wi_hbm, g1_hbm, tw_hbm, o_ref,
    sw_ref, skip_ref, tw_ref, qkv, filt, f1, w, wi, g1, tail, ends, halo, ht, dt, hr, xr, ys, lt, drive, query, spec, b, y, g,
    load_sem, halo_sem, send_sem, recv_sem,
):
    me = lax.axis_index("seq")
    ch = lax.axis_index("ch")
    tok = qkv.shape[1]
    chans = qkv.shape[2]
    rows = parts * R
    lines = parts * C
    chunks = chans // lines
    half = tok // 2

    lanes = [pl.ds(chunk * lines, lines) for chunk in range(chunks)]
    loads = [
        pltpu.make_async_copy(src, dst, load_sem.at[i])
        for i, (src, dst) in enumerate(
            [(filt_hbm.at[:, at], filt.at[:, at]) for at in lanes]
            + [(qkv_hbm.at[:, pl.ds(tok - 16, 16), :], tail)]
            + [(qkv_hbm, qkv), (sw_hbm, sw_ref), (skip_hbm, skip_ref), (tw_hbm, tw_ref), (f1_hbm, f1), (w_hbm, w), (wi_hbm, wi), (g1_hbm, g1)]
        )
    ]

    barrier = pltpu.get_barrier_semaphore()

    z, x, core = me >> 3, (me >> 1) & 3, me & 1

    def tour(steps, visit, side=None):
        for flip in range(2):
            for some in (steps[:8], steps[8:]):
                code = sum((4 * dz + dx) << (4 * i) for i, (dz, dx) in enumerate(some))
                code = code - 2**32 if code >= 2**31 else code

                def one(k, carry):
                    step = (jnp.int32(code) >> (4 * k)) & 15
                    visit((((z + (step >> 2)) & 3) << 3) + (((x + step) & 3) << 1) + ((core ^ flip) if side is None else (side ^ flip)))
                    return carry

                lax.fori_loop(0, len(some), one, 0)
        visit(me ^ 1)

    def greet(to):
        pl.semaphore_signal(barrier, inc=1, device_id=(to, ch), device_id_type=MESH)

    tour(STEPS, greet)
    for load in loads[: chunks + 1]:
        load.start()

    def turn(dst, j, value):
        value = value.T
        for d in range(128 // C):
            mine = value[d * C : (d + 1) * C, :]
            message = jnp.concatenate([mine[:, :half], mine[:, half:]], axis=0).astype(BF16)
            dst[pl.ds(pl.multiple_of(j * 128 * R // C + d * R, R), R), :] = message

    def turn_filter(j, carry):
        turn(ht, j, filt[:, pl.ds(pl.multiple_of(j * 128, 128), 128)])
        return carry

    loads[0].wait()
    lax.fori_loop(0, lines // 128, turn_filter, 0)
    loads[chunks].wait()
    last = [tail[m].astype(F32)[14:, :] for m in range(3)]
    ends[...] = jnp.concatenate(last + [jnp.zeros((10, chans), F32)], axis=0).astype(BF16)
    pl.semaphore_wait(barrier, parts - 1)

    edge = pltpu.make_async_remote_copy(
        src_ref=ends, dst_ref=halo, send_sem=halo_sem.at[0], recv_sem=halo_sem.at[1],
        device_id=((me + 1) & (parts - 1), ch), device_id_type=MESH,
    )
    edge.start()

    def deal(kind, chunk, src, dst):
        base = chunk * rows

        def send(to):
            pltpu.make_async_remote_copy(
                src_ref=src.at[pl.ds(pl.multiple_of(base + to * R, R), R), :],
                dst_ref=dst.at[pl.ds(pl.multiple_of(base + me * R, R), R), :],
                send_sem=send_sem.at[kind, chunk],
                recv_sem=recv_sem.at[kind, chunk],
                device_id=(to, ch),
                device_id_type=MESH,
            ).start()

        tour(STEPS, send, 1 if kind == 2 else None)
        own = pl.ds(pl.multiple_of(base + me * R, R), R)
        pltpu.make_async_copy(src.at[own, :], dst.at[own, :], recv_sem.at[kind, chunk]).start()

    def arrived(kind, chunk, dst):
        whole = dst.at[pl.ds(pl.multiple_of(chunk * rows, rows), rows), :]
        pltpu.make_async_copy(whole, whole, recv_sem.at[kind, chunk]).wait()

    def left(kind, chunk, src):
        sent = src.at[pl.ds(0, rows - R), :]
        pltpu.make_async_copy(sent, sent, send_sem.at[kind, chunk]).wait()

    deal(0, 0, ht, hr)
    for load in loads[chunks + 1 :]:
        load.start()
    loads[chunks + 1].wait()
    loads[chunks + 2].wait()
    edge.wait_recv()
    first = jnp.where(me > 0, 1.0, 0.0).astype(F32)

    def short(m, at):
        before = halo[:, at].astype(F32)[2 * m : 2 * m + 2, :] * first
        before = jnp.concatenate([jnp.zeros((6, 128), F32), before], axis=0)
        ext = jnp.concatenate([before, qkv[m, :, at].astype(F32)], axis=0)
        return (
            sw_ref[m, 0:1, at] * ext[8:, :]
            + sw_ref[m, 1:2, at] * ext[7:-1, :]
            + sw_ref[m, 2:3, at] * ext[6:-2, :]
        )

    for chunk in range(chunks):

        def gate(j, carry):
            at = pl.ds(pl.multiple_of(j * 128, 128), 128)
            value = short(1, at) * short(2, at)
            drive[:, at] = value
            turn(dt, j, value)
            return carry

        if chunk:
            loads[chunk].wait()
            lax.fori_loop(chunk * lines // 128, (chunk + 1) * lines // 128, turn_filter, 0)
            deal(0, chunk, ht, hr)
        lax.fori_loop(chunk * lines // 128, (chunk + 1) * lines // 128, gate, 0)
        deal(1, chunk, dt, xr)

    def ask(j, carry):
        at = pl.ds(pl.multiple_of(j * 128, 128), 128)
        query[:, at] = short(0, at)
        return carry

    lax.fori_loop(0, chans // 128, ask, 0)

    def split(m_ref, at, value):
        return dot(m_ref[0, at, :], value) + dot(m_ref[1, at, :], value)

    def along_parts(blocks):
        real, imag = split(f1, slice(0, rows), blocks), split(f1, slice(rows, 2 * rows), blocks)
        for k in range(0, parts, 2):
            for n in range(2):
                at = slice(n * half, (n + 1) * half)
                turned = []
                for p in (k, k + 1):
                    cos, sin = tw_ref[0, p : p + 1, at], tw_ref[1, p : p + 1, at]
                    here = slice(p * R + n * C, p * R + (n + 1) * C)
                    re, im = real[here, :], imag[here, :]
                    turned.append((re * cos + im * sin, im * cos - re * sin))
                b[k * C : (k + 2) * C, n * half : (n + 1) * half] = jnp.concatenate(
                    [t[0] for t in turned], axis=0
                ).astype(BF16)
                b[k * C : (k + 2) * C, tok + n * half : tok + (n + 1) * half] = jnp.concatenate(
                    [t[1] for t in turned], axis=0
                ).astype(BF16)

    for load in loads[chunks + 3 :]:
        load.wait()

    def place(chunk):
        return pl.ds(pl.multiple_of(chunk * rows, rows), rows)

    def filter_spectra(chunk):
        arrived(0, chunk, hr)
        along_parts(hr[place(chunk), :])
        for n in range(4):
            spec[:, n * half : (n + 1) * half] = dot(b[...], w[:, n * half : (n + 1) * half])

    def convolve(chunk):
        arrived(1, chunk, xr)
        along_parts(xr[place(chunk), :])
        for n in range(2):
            real_at, imag_at = slice(n * half, (n + 1) * half), slice(tok + n * half, tok + (n + 1) * half)
            xre, xim = dot(b[...], w[:, real_at]), dot(b[...], w[:, imag_at])
            hre, him = spec[:, real_at], spec[:, imag_at]
            y[:, real_at] = (xre * hre - xim * him).astype(BF16)
            y[:, imag_at] = (xre * him + xim * hre).astype(BF16)
        back = [dot(y[...], wi[:, n * half : (n + 1) * half]) for n in range(4)]
        scale = 2.0 / (2 * parts * tok)
        for k in range(parts):
            turned = []
            for n in range(2):
                at = slice(n * half, (n + 1) * half)
                cos, sin = tw_ref[0, k : k + 1, at] * scale, tw_ref[1, k : k + 1, at] * scale
                re, im = back[n][k * C : (k + 1) * C, :], back[2 + n][k * C : (k + 1) * C, :]
                turned.append((re * cos - im * sin, im * cos + re * sin))
            for part in range(2):
                g[part * rows + k * R : part * rows + (k + 1) * R, :] = jnp.concatenate(
                    [t[part] for t in turned], axis=0
                ).astype(BF16)
        ys[place(chunk), :] = split(g1, slice(0, rows), g[...]).astype(BF16)

    def one_chunk(chunk, carry):
        filter_spectra(chunk)
        convolve(chunk)
        deal(2, chunk, ys, lt)
        return carry

    lax.fori_loop(0, chunks, one_chunk, 0)

    def finish(j, carry):
        at = pl.ds(pl.multiple_of(j * 128, 128), 128)
        came = lt[pl.ds(pl.multiple_of(j * 128 * R // C, 128 * R // C), 128 * R // C), :].astype(F32)
        for n in range(2):
            long_part = jnp.concatenate(
                [came[d * R + n * C : d * R + (n + 1) * C, :] for d in range(128 // C)], axis=0
            ).T
            here = slice(n * half, (n + 1) * half)
            o_ref[here, at] = (
                query[here, at] * (long_part + skip_ref[0:1, at] * drive[here, at])
            ).astype(BF16)
        return carry

    for chunk in range(chunks):
        arrived(2, chunk, lt)
        lax.fori_loop(chunk * lines // 128, (chunk + 1) * lines // 128, finish, 0)

    edge.wait_send()
    for chunk in range(chunks):
        left(0, chunk, ht)
        left(1, chunk, dt)
        left(2, chunk, ys)


def solution(mesh):
    parts = mesh.shape["seq"]

    def on_device(qkv, short_weight, long_filter, skip):
        tok, chans = long_filter.shape
        rows, lines = parts * R, parts * C
        chunks = chans // lines
        f1, w, wi, g1, tw = tables(parts, tok)
        vmem = pl.BlockSpec(memory_space=pltpu.VMEM)
        hbm = pl.BlockSpec(memory_space=pl.ANY)
        return pl.pallas_call(
            functools.partial(kernel, parts),
            out_shape=pltpu.VMEM((tok, chans), BF16),
            in_specs=[hbm] * 9,
            out_specs=vmem,
            scratch_shapes=[
                pltpu.VMEM(short_weight.shape, F32),
                pltpu.VMEM((1, chans), F32),
                pltpu.VMEM(tw.shape, F32),
                pltpu.VMEM(qkv.shape, BF16),
                pltpu.VMEM((tok, chans), F32),
                pltpu.VMEM(f1.shape, BF16),
                pltpu.VMEM(w.shape, BF16),
                pltpu.VMEM(wi.shape, BF16),
                pltpu.VMEM(g1.shape, BF16),
                pltpu.VMEM((3, 16, chans), BF16),
                pltpu.VMEM((16, chans), BF16),
                pltpu.VMEM((16, chans), BF16),
                pltpu.VMEM((chunks * rows, tok // 2), BF16),
                pltpu.VMEM((chunks * rows, tok // 2), BF16),
                pltpu.VMEM((chunks * rows, tok // 2), BF16),
                pltpu.VMEM((chunks * rows, tok // 2), BF16),
                pltpu.VMEM((chunks * rows, tok // 2), BF16),
                pltpu.VMEM((chunks * rows, tok // 2), BF16),
                pltpu.VMEM((tok, chans), F32),
                pltpu.VMEM((tok, chans), F32),
                pltpu.VMEM((lines, 2 * tok), F32),
                pltpu.VMEM((lines, 2 * tok), BF16),
                pltpu.VMEM((lines, 2 * tok), BF16),
                pltpu.VMEM((2 * rows, tok // 2), BF16),
                pltpu.SemaphoreType.DMA((chunks + 9,)),
                pltpu.SemaphoreType.DMA((2,)),
                pltpu.SemaphoreType.DMA((3, chunks)),
                pltpu.SemaphoreType.DMA((3, chunks)),
            ],
            compiler_params=pltpu.CompilerParams(
                collective_id=0, has_side_effects=True, vmem_limit_bytes=60 * 2**20
            ),
        )(qkv, short_weight, long_filter, skip[None, :], f1, w, wi, g1, tw)

    return jax.shard_map(
        on_device,
        mesh=mesh,
        in_specs=(P(None, "seq", "ch"), P(None, None, "ch"), P("seq", "ch"), P("ch")),
        out_specs=P("seq", "ch"),
        check_vma=False,
    )
```

```python
import functools

import jax
import jax.numpy as jnp
import numpy as np
from jax import lax
from jax.experimental import pallas as pl
from jax.experimental.pallas import tpu as pltpu
from jax.sharding import PartitionSpec as P

MESH = pl.DeviceIdType.MESH
C = 8
R = 16
STEPS = ((2, 2), (2, 1), (1, 2), (2, 3), (3, 2), (1, 1), (3, 3), (1, 3), (3, 1), (2, 0), (0, 2), (0, 1), (1, 0), (0, 3), (3, 0))
F32 = jnp.float32
BF16 = jnp.bfloat16


def dot(a, b):
    return jnp.dot(a, b, preferred_element_type=F32)


def tables(parts, tok):
    place = np.arange(parts)
    odd = 2 * place + 1
    angle = 2 * np.pi * np.outer(odd, place) / (4 * parts)
    spread = lambda m: np.kron(m, np.eye(R))
    f1 = np.concatenate([spread(np.cos(angle)), spread(-np.sin(angle))], axis=0)
    g1 = np.concatenate([spread(np.cos(angle).T), spread(-np.sin(angle).T)], axis=1)
    offset = np.arange(tok)
    angle = 2 * np.pi * (np.outer(offset, offset) % tok) / tok
    cos, sin = np.cos(angle), np.sin(angle)
    w = np.block([[cos, -sin], [sin, cos]])
    wi = np.block([[cos, sin], [-sin, cos]])
    angle = 2 * np.pi * np.outer(odd, offset) / (4 * parts * tok)
    tw = np.stack([np.cos(angle), np.sin(angle)])
    half = lambda m: m.astype(np.float32).astype(BF16)
    rest = lambda m: half(m - half(m).astype(np.float64))
    f1 = np.stack([half(f1), rest(f1)])
    g1 = np.stack([half(g1), rest(g1)])
    return f1, np.stack([half(w), rest(w)]), half(wi), g1, tw.astype(np.float32)


def kernel(
    parts, qkv_hbm, sw_hbm, filt_hbm, skip_hbm, f1_hbm, w_hbm, wi_hbm, g1_hbm, tw_hbm, o_ref,
    sw_ref, skip_ref, tw_ref, qkv, filt, f1, w, wi, g1, tail, ends, halo, ht, dt, hr, xr, ys, lt, drive, query, spec, b, y, g,
    load_sem, halo_sem, send_sem, recv_sem,
):
    me = lax.axis_index("seq")
    ch = lax.axis_index("ch")
    tok = qkv.shape[1]
    chans = qkv.shape[2]
    rows = parts * R
    lines = parts * C
    chunks = chans // lines
    half = tok // 2

    lanes = [pl.ds(chunk * lines, lines) for chunk in range(chunks)]
    loads = [
        pltpu.make_async_copy(src, dst, load_sem.at[i])
        for i, (src, dst) in enumerate(
            [(filt_hbm.at[:, at], filt.at[:, at]) for at in lanes]
            + [(qkv_hbm.at[:, pl.ds(tok - 16, 16), :], tail)]
            + [(qkv_hbm, qkv), (sw_hbm, sw_ref), (skip_hbm, skip_ref), (tw_hbm, tw_ref), (f1_hbm, f1), (w_hbm, w), (wi_hbm, wi), (g1_hbm, g1)]
        )
    ]

    barrier = pltpu.get_barrier_semaphore()

    z, x, core = me >> 3, (me >> 1) & 3, me & 1

    def tour(steps, visit, side=None):
        for flip in range(2):
            for some in (steps[:8], steps[8:]):
                code = sum((4 * dz + dx) << (4 * i) for i, (dz, dx) in enumerate(some))
                code = code - 2**32 if code >= 2**31 else code

                def one(k, carry):
                    step = (jnp.int32(code) >> (4 * k)) & 15
                    visit((((z + (step >> 2)) & 3) << 3) + (((x + step) & 3) << 1) + ((core ^ flip) if side is None else (side ^ flip)))
                    return carry

                lax.fori_loop(0, len(some), one, 0, unroll=True)
        visit(me ^ 1)

    def greet(to):
        pl.semaphore_signal(barrier, inc=1, device_id=(to, ch), device_id_type=MESH)

    tour(STEPS, greet)
    for load in loads[: chunks + 1]:
        load.start()

    def turn(dst, j, value):
        value = value.T
        for d in range(128 // C):
            mine = value[d * C : (d + 1) * C, :]
            message = jnp.concatenate([mine[:, :half], mine[:, half:]], axis=0).astype(BF16)
            dst[pl.ds(pl.multiple_of(j * 128 * R // C + d * R, R), R), :] = message

    def turn_filter(j, carry):
        turn(ht, j, filt[:, pl.ds(pl.multiple_of(j * 128, 128), 128)])
        return carry

    loads[0].wait()
    lax.fori_loop(0, lines // 128, turn_filter, 0)
    loads[chunks].wait()
    last = [tail[m].astype(F32)[14:, :] for m in range(3)]
    ends[...] = jnp.concatenate(last + [jnp.zeros((10, chans), F32)], axis=0).astype(BF16)
    pl.semaphore_wait(barrier, parts - 1)

    edge = pltpu.make_async_remote_copy(
        src_ref=ends, dst_ref=halo, send_sem=halo_sem.at[0], recv_sem=halo_sem.at[1],
        device_id=((me + 1) & (parts - 1), ch), device_id_type=MESH,
    )
    edge.start()

    def deal(kind, chunk, src, dst):
        base = chunk * rows

        def send(to):
            pltpu.make_async_remote_copy(
                src_ref=src.at[pl.ds(pl.multiple_of(base + to * R, R), R), :],
                dst_ref=dst.at[pl.ds(pl.multiple_of(base + me * R, R), R), :],
                send_sem=send_sem.at[kind, chunk],
                recv_sem=recv_sem.at[kind, chunk],
                device_id=(to, ch),
                device_id_type=MESH,
            ).start()

        tour(STEPS, send, 1 if kind == 2 else None)
        own = pl.ds(pl.multiple_of(base + me * R, R), R)
        pltpu.make_async_copy(src.at[own, :], dst.at[own, :], recv_sem.at[kind, chunk]).start()

    def arrived(kind, chunk, dst):
        whole = dst.at[pl.ds(pl.multiple_of(chunk * rows, rows), rows), :]
        pltpu.make_async_copy(whole, whole, recv_sem.at[kind, chunk]).wait()

    def left(kind, chunk, src):
        sent = src.at[pl.ds(0, rows - R), :]
        pltpu.make_async_copy(sent, sent, send_sem.at[kind, chunk]).wait()

    deal(0, 0, ht, hr)
    for load in loads[chunks + 1 :]:
        load.start()
    loads[chunks + 1].wait()
    loads[chunks + 2].wait()
    edge.wait_recv()
    first = jnp.where(me > 0, 1.0, 0.0).astype(F32)

    def short(m, at):
        before = halo[:, at].astype(F32)[2 * m : 2 * m + 2, :] * first
        before = jnp.concatenate([jnp.zeros((6, 128), F32), before], axis=0)
        ext = jnp.concatenate([before, qkv[m, :, at].astype(F32)], axis=0)
        return (
            sw_ref[m, 0:1, at] * ext[8:, :]
            + sw_ref[m, 1:2, at] * ext[7:-1, :]
            + sw_ref[m, 2:3, at] * ext[6:-2, :]
        )

    for chunk in range(chunks):

        def gate(j, carry):
            at = pl.ds(pl.multiple_of(j * 128, 128), 128)
            value = short(1, at) * short(2, at)
            drive[:, at] = value
            turn(dt, j, value)
            return carry

        if chunk:
            loads[chunk].wait()
            lax.fori_loop(chunk * lines // 128, (chunk + 1) * lines // 128, turn_filter, 0)
            deal(0, chunk, ht, hr)
        lax.fori_loop(chunk * lines // 128, (chunk + 1) * lines // 128, gate, 0)
        deal(1, chunk, dt, xr)

    def ask(j, carry):
        at = pl.ds(pl.multiple_of(j * 128, 128), 128)
        query[:, at] = short(0, at)
        return carry

    lax.fori_loop(0, chans // 128, ask, 0)

    def split(m_ref, at, value):
        return dot(m_ref[0, at, :], value) + dot(m_ref[1, at, :], value)

    def along_parts(blocks):
        real, imag = split(f1, slice(0, rows), blocks), split(f1, slice(rows, 2 * rows), blocks)
        for k in range(0, parts, 2):
            for n in range(2):
                at = slice(n * half, (n + 1) * half)
                turned = []
                for p in (k, k + 1):
                    cos, sin = tw_ref[0, p : p + 1, at], tw_ref[1, p : p + 1, at]
                    here = slice(p * R + n * C, p * R + (n + 1) * C)
                    re, im = real[here, :], imag[here, :]
                    turned.append((re * cos + im * sin, im * cos - re * sin))
                b[k * C : (k + 2) * C, n * half : (n + 1) * half] = jnp.concatenate(
                    [t[0] for t in turned], axis=0
                ).astype(BF16)
                b[k * C : (k + 2) * C, tok + n * half : tok + (n + 1) * half] = jnp.concatenate(
                    [t[1] for t in turned], axis=0
                ).astype(BF16)

    for load in loads[chunks + 3 :]:
        load.wait()

    def place(chunk):
        return pl.ds(pl.multiple_of(chunk * rows, rows), rows)

    def filter_spectra(chunk):
        arrived(0, chunk, hr)
        along_parts(hr[place(chunk), :])
        for n in range(4):
            spec[:, n * half : (n + 1) * half] = dot(b[...], w[0, :, n * half : (n + 1) * half]) + dot(b[...], w[1, :, n * half : (n + 1) * half])

    def convolve(chunk):
        arrived(1, chunk, xr)
        along_parts(xr[place(chunk), :])
        for n in range(2):
            real_at, imag_at = slice(n * half, (n + 1) * half), slice(tok + n * half, tok + (n + 1) * half)
            xre, xim = dot(b[...], w[0, :, real_at]), dot(b[...], w[0, :, imag_at])
            hre, him = spec[:, real_at], spec[:, imag_at]
            y[:, real_at] = (xre * hre - xim * him).astype(BF16)
            y[:, imag_at] = (xre * him + xim * hre).astype(BF16)
        back = [dot(y[...], wi[:, n * half : (n + 1) * half]) for n in range(4)]
        scale = 2.0 / (2 * parts * tok)
        for k in range(parts):
            turned = []
            for n in range(2):
                at = slice(n * half, (n + 1) * half)
                cos, sin = tw_ref[0, k : k + 1, at] * scale, tw_ref[1, k : k + 1, at] * scale
                re, im = back[n][k * C : (k + 1) * C, :], back[2 + n][k * C : (k + 1) * C, :]
                turned.append((re * cos - im * sin, im * cos + re * sin))
            for part in range(2):
                g[part * rows + k * R : part * rows + (k + 1) * R, :] = jnp.concatenate(
                    [t[part] for t in turned], axis=0
                ).astype(BF16)
        ys[place(chunk), :] = split(g1, slice(0, rows), g[...]).astype(BF16)

    def one_chunk(chunk, carry):
        filter_spectra(chunk)
        convolve(chunk)
        deal(2, chunk, ys, lt)
        return carry

    lax.fori_loop(0, chunks, one_chunk, 0)

    def finish(j, carry):
        at = pl.ds(pl.multiple_of(j * 128, 128), 128)
        came = lt[pl.ds(pl.multiple_of(j * 128 * R // C, 128 * R // C), 128 * R // C), :].astype(F32)
        for n in range(2):
            long_part = jnp.concatenate(
                [came[d * R + n * C : d * R + (n + 1) * C, :] for d in range(128 // C)], axis=0
            ).T
            here = slice(n * half, (n + 1) * half)
            o_ref[here, at] = (
                query[here, at] * (long_part + skip_ref[0:1, at] * drive[here, at])
            ).astype(BF16)
        return carry

    for chunk in range(chunks):
        arrived(2, chunk, lt)
        lax.fori_loop(chunk * lines // 128, (chunk + 1) * lines // 128, finish, 0)

    edge.wait_send()
    for chunk in range(chunks):
        left(0, chunk, ht)
        left(1, chunk, dt)
        left(2, chunk, ys)


def solution(mesh):
    parts = mesh.shape["seq"]

    def on_device(qkv, short_weight, long_filter, skip):
        tok, chans = long_filter.shape
        rows, lines = parts * R, parts * C
        chunks = chans // lines
        f1, w, wi, g1, tw = tables(parts, tok)
        vmem = pl.BlockSpec(memory_space=pltpu.VMEM)
        hbm = pl.BlockSpec(memory_space=pl.ANY)
        return pl.pallas_call(
            functools.partial(kernel, parts),
            out_shape=pltpu.VMEM((tok, chans), BF16),
            in_specs=[hbm] * 9,
            out_specs=vmem,
            scratch_shapes=[
                pltpu.VMEM(short_weight.shape, F32),
                pltpu.VMEM((1, chans), F32),
                pltpu.VMEM(tw.shape, F32),
                pltpu.VMEM(qkv.shape, BF16),
                pltpu.VMEM((tok, chans), F32),
                pltpu.VMEM(f1.shape, BF16),
                pltpu.VMEM(w.shape, BF16),
                pltpu.VMEM(wi.shape, BF16),
                pltpu.VMEM(g1.shape, BF16),
                pltpu.VMEM((3, 16, chans), BF16),
                pltpu.VMEM((16, chans), BF16),
                pltpu.VMEM((16, chans), BF16),
                pltpu.VMEM((chunks * rows, tok // 2), BF16),
                pltpu.VMEM((chunks * rows, tok // 2), BF16),
                pltpu.VMEM((chunks * rows, tok // 2), BF16),
                pltpu.VMEM((chunks * rows, tok // 2), BF16),
                pltpu.VMEM((chunks * rows, tok // 2), BF16),
                pltpu.VMEM((chunks * rows, tok // 2), BF16),
                pltpu.VMEM((tok, chans), F32),
                pltpu.VMEM((tok, chans), F32),
                pltpu.VMEM((lines, 2 * tok), F32),
                pltpu.VMEM((lines, 2 * tok), BF16),
                pltpu.VMEM((lines, 2 * tok), BF16),
                pltpu.VMEM((2 * rows, tok // 2), BF16),
                pltpu.SemaphoreType.DMA((chunks + 9,)),
                pltpu.SemaphoreType.DMA((2,)),
                pltpu.SemaphoreType.DMA((3, chunks)),
                pltpu.SemaphoreType.DMA((3, chunks)),
            ],
            compiler_params=pltpu.CompilerParams(
                collective_id=0, has_side_effects=True, vmem_limit_bytes=60 * 2**20
            ),
        )(qkv, short_weight, long_filter, skip[None, :], f1, w, wi, g1, tw)

    return jax.shard_map(
        on_device,
        mesh=mesh,
        in_specs=(P(None, "seq", "ch"), P(None, None, "ch"), P("seq", "ch"), P("ch")),
        out_specs=P("seq", "ch"),
        check_vma=False,
    )
```

```python
import functools

import jax
import jax.numpy as jnp
import numpy as np
from jax import lax
from jax.experimental import pallas as pl
from jax.experimental.pallas import tpu as pltpu
from jax.sharding import PartitionSpec as P

MESH = pl.DeviceIdType.MESH
C = 8
R = 16
STEPS = ((2, 2), (2, 1), (1, 2), (2, 3), (3, 2), (1, 1), (3, 3), (1, 3), (3, 1), (2, 0), (0, 2), (0, 1), (1, 0), (0, 3), (3, 0))
F32 = jnp.float32
BF16 = jnp.bfloat16


def dot(a, b):
    return jnp.dot(a, b, preferred_element_type=F32)


def tables(parts, tok):
    place = np.arange(parts)
    odd = 2 * place + 1
    angle = 2 * np.pi * np.outer(odd, place) / (4 * parts)
    spread = lambda m: np.kron(m, np.eye(R))
    f1 = np.concatenate([spread(np.cos(angle)), spread(-np.sin(angle))], axis=0)
    g1 = np.concatenate([spread(np.cos(angle).T), spread(-np.sin(angle).T)], axis=1)
    offset = np.arange(tok)
    angle = 2 * np.pi * (np.outer(offset, offset) % tok) / tok
    cos, sin = np.cos(angle), np.sin(angle)
    w = np.block([[cos, -sin], [sin, cos]])
    wi = np.block([[cos, sin], [-sin, cos]])
    angle = 2 * np.pi * np.outer(odd, offset) / (4 * parts * tok)
    tw = np.stack([np.cos(angle), np.sin(angle)])
    half = lambda m: m.astype(np.float32).astype(BF16)
    rest = lambda m: half(m - half(m).astype(np.float64))
    f1 = np.stack([half(f1), rest(f1)])
    g1 = np.stack([half(g1), rest(g1)])
    return f1, np.stack([half(w), rest(w)]), half(wi), g1, tw.astype(np.float32)


def kernel(
    parts, qkv_hbm, sw_hbm, filt_hbm, skip_hbm, f1_hbm, w_hbm, wi_hbm, g1_hbm, tw_hbm, o_ref,
    sw_ref, skip_ref, tw_ref, qkv, filt, f1, w, wi, g1, tail, ends, halo, before, ht, dt, hr, xr, ys, lt, drive, query, spec, b, y, g,
    load_sem, halo_sem, send_sem, recv_sem,
):
    me = lax.axis_index("seq")
    ch = lax.axis_index("ch")
    tok = qkv.shape[1]
    chans = qkv.shape[2]
    rows = parts * R
    lines = parts * C
    chunks = chans // lines
    half = tok // 2

    lanes = [pl.ds(chunk * lines, lines) for chunk in range(chunks)]
    loads = [
        pltpu.make_async_copy(src, dst, load_sem.at[i])
        for i, (src, dst) in enumerate(
            [(filt_hbm.at[:, at], filt.at[:, at]) for at in lanes]
            + [(qkv_hbm.at[:, pl.ds(tok - 16, 16), :], tail)]
            + [(qkv_hbm, qkv), (sw_hbm, sw_ref), (skip_hbm, skip_ref), (tw_hbm, tw_ref), (f1_hbm, f1), (w_hbm, w), (wi_hbm, wi), (g1_hbm, g1)]
        )
    ]

    barrier = pltpu.get_barrier_semaphore()

    z, x, core = me >> 3, (me >> 1) & 3, me & 1

    def tour(steps, visit, side=None):
        for flip in range(2):
            for some in (steps[:8], steps[8:]):
                code = sum((4 * dz + dx) << (4 * i) for i, (dz, dx) in enumerate(some))
                code = code - 2**32 if code >= 2**31 else code

                def one(k, carry):
                    step = (jnp.int32(code) >> (4 * k)) & 15
                    visit((((z + (step >> 2)) & 3) << 3) + (((x + step) & 3) << 1) + ((core ^ flip) if side is None else (side ^ flip)))
                    return carry

                lax.fori_loop(0, len(some), one, 0, unroll=True)
        visit(me ^ 1)

    def greet(to):
        pl.semaphore_signal(barrier, inc=1, device_id=(to, ch), device_id_type=MESH)

    tour(STEPS, greet)
    for load in loads[: chunks + 1]:
        load.start()

    def turn(dst, j, value):
        value = value.T
        for d in range(128 // C):
            mine = value[d * C : (d + 1) * C, :]
            message = jnp.concatenate([mine[:, :half], mine[:, half:]], axis=0).astype(BF16)
            dst[pl.ds(pl.multiple_of(j * 128 * R // C + d * R, R), R), :] = message

    def turn_filter(j, carry):
        turn(ht, j, filt[:, pl.ds(pl.multiple_of(j * 128, 128), 128)])
        return carry

    loads[0].wait()
    lax.fori_loop(0, lines // 128, turn_filter, 0, unroll=True)
    loads[chunks].wait()
    last = [tail[m].astype(F32)[14:, :] for m in range(3)]
    last = [row[:, at : at + chans // 2] for row in last for at in (0, chans // 2)]
    ends[...] = jnp.concatenate(last + [jnp.zeros((4, chans // 2), F32)], axis=0).astype(BF16)
    pl.semaphore_wait(barrier, parts - 1)

    edge = pltpu.make_async_remote_copy(
        src_ref=ends, dst_ref=halo, send_sem=halo_sem.at[0], recv_sem=halo_sem.at[1],
        device_id=((me + 1) & (parts - 1), ch), device_id_type=MESH,
    )
    edge.start()

    def deal(kind, chunk, src, dst):
        base = chunk * rows

        def send(to):
            pltpu.make_async_remote_copy(
                src_ref=src.at[pl.ds(pl.multiple_of(base + to * R, R), R), :],
                dst_ref=dst.at[pl.ds(pl.multiple_of(base + me * R, R), R), :],
                send_sem=send_sem.at[kind, chunk],
                recv_sem=recv_sem.at[kind, chunk],
                device_id=(to, ch),
                device_id_type=MESH,
            ).start()

        tour(STEPS, send, 1 if kind == 2 else None)
        own = pl.ds(pl.multiple_of(base + me * R, R), R)
        pltpu.make_async_copy(src.at[own, :], dst.at[own, :], recv_sem.at[kind, chunk]).start()

    def arrived(kind, chunk, dst):
        whole = dst.at[pl.ds(pl.multiple_of(chunk * rows, rows), rows), :]
        pltpu.make_async_copy(whole, whole, recv_sem.at[kind, chunk]).wait()

    def left(kind, chunk, src):
        sent = src.at[pl.ds(0, rows - R), :]
        pltpu.make_async_copy(sent, sent, send_sem.at[kind, chunk]).wait()

    deal(0, 0, ht, hr)
    for load in loads[chunks + 1 :]:
        load.start()
    loads[chunks + 1].wait()
    loads[chunks + 2].wait()
    edge.wait_recv()
    ended = halo[...].astype(F32)
    for m in range(3):
        both = [ended[4 * m + 2 * n : 4 * m + 2 * n + 2, :] for n in range(2)]
        both = jnp.concatenate([jnp.concatenate(both, axis=1), jnp.zeros((6, chans), F32)], axis=0)
        before[m] = both * jnp.where(me > 0, 1.0, 0.0).astype(F32)

    def short(m, at):
        above = jnp.concatenate([jnp.zeros((6, 128), F32), before[m, :2, at]], axis=0)
        ext = jnp.concatenate([above, qkv[m, :, at].astype(F32)], axis=0)
        return (
            sw_ref[m, 0:1, at] * ext[8:, :]
            + sw_ref[m, 1:2, at] * ext[7:-1, :]
            + sw_ref[m, 2:3, at] * ext[6:-2, :]
        )

    for chunk in range(chunks):

        def gate(j, carry):
            at = pl.ds(pl.multiple_of(j * 128, 128), 128)
            value = short(1, at) * short(2, at)
            drive[:, at] = value
            turn(dt, j, value)
            return carry

        if chunk:
            loads[chunk].wait()
            lax.fori_loop(chunk * lines // 128, (chunk + 1) * lines // 128, turn_filter, 0, unroll=True)
            deal(0, chunk, ht, hr)
        lax.fori_loop(chunk * lines // 128, (chunk + 1) * lines // 128, gate, 0, unroll=True)
        deal(1, chunk, dt, xr)

    def ask(j, carry):
        at = pl.ds(pl.multiple_of(j * 128, 128), 128)
        query[:, at] = short(0, at)
        return carry

    lax.fori_loop(0, chans // 128, ask, 0)

    def split(m_ref, at, value):
        return dot(m_ref[0, at, :], value) + dot(m_ref[1, at, :], value)

    def along_parts(blocks):
        real, imag = split(f1, slice(0, rows), blocks), split(f1, slice(rows, 2 * rows), blocks)
        for k in range(0, parts, 2):
            for n in range(2):
                at = slice(n * half, (n + 1) * half)
                turned = []
                for p in (k, k + 1):
                    cos, sin = tw_ref[0, p : p + 1, at], tw_ref[1, p : p + 1, at]
                    here = slice(p * R + n * C, p * R + (n + 1) * C)
                    re, im = real[here, :], imag[here, :]
                    turned.append((re * cos + im * sin, im * cos - re * sin))
                b[k * C : (k + 2) * C, n * half : (n + 1) * half] = jnp.concatenate(
                    [t[0] for t in turned], axis=0
                ).astype(BF16)
                b[k * C : (k + 2) * C, tok + n * half : tok + (n + 1) * half] = jnp.concatenate(
                    [t[1] for t in turned], axis=0
                ).astype(BF16)

    for load in loads[chunks + 3 :]:
        load.wait()

    def place(chunk):
        return pl.ds(pl.multiple_of(chunk * rows, rows), rows)

    def filter_spectra(chunk):
        arrived(0, chunk, hr)
        along_parts(hr[place(chunk), :])
        for n in range(4):
            spec[:, n * half : (n + 1) * half] = dot(b[...], w[0, :, n * half : (n + 1) * half]) + dot(b[...], w[1, :, n * half : (n + 1) * half])

    def convolve(chunk):
        arrived(1, chunk, xr)
        along_parts(xr[place(chunk), :])
        for n in range(2):
            real_at, imag_at = slice(n * half, (n + 1) * half), slice(tok + n * half, tok + (n + 1) * half)
            xre, xim = dot(b[...], w[0, :, real_at]), dot(b[...], w[0, :, imag_at])
            hre, him = spec[:, real_at], spec[:, imag_at]
            y[:, real_at] = (xre * hre - xim * him).astype(BF16)
            y[:, imag_at] = (xre * him + xim * hre).astype(BF16)
        back = [dot(y[...], wi[:, n * half : (n + 1) * half]) for n in range(4)]
        scale = 2.0 / (2 * parts * tok)
        for k in range(parts):
            turned = []
            for n in range(2):
                at = slice(n * half, (n + 1) * half)
                cos, sin = tw_ref[0, k : k + 1, at] * scale, tw_ref[1, k : k + 1, at] * scale
                re, im = back[n][k * C : (k + 1) * C, :], back[2 + n][k * C : (k + 1) * C, :]
                turned.append((re * cos - im * sin, im * cos + re * sin))
            for part in range(2):
                g[part * rows + k * R : part * rows + (k + 1) * R, :] = jnp.concatenate(
                    [t[part] for t in turned], axis=0
                ).astype(BF16)
        ys[place(chunk), :] = split(g1, slice(0, rows), g[...]).astype(BF16)

    def one_chunk(chunk, carry):
        filter_spectra(chunk)
        convolve(chunk)
        deal(2, chunk, ys, lt)
        return carry

    lax.fori_loop(0, chunks, one_chunk, 0)

    def finish(j, carry):
        at = pl.ds(pl.multiple_of(j * 128, 128), 128)
        came = lt[pl.ds(pl.multiple_of(j * 128 * R // C, 128 * R // C), 128 * R // C), :].astype(F32)
        for n in range(2):
            long_part = jnp.concatenate(
                [came[d * R + n * C : d * R + (n + 1) * C, :] for d in range(128 // C)], axis=0
            ).T
            here = slice(n * half, (n + 1) * half)
            o_ref[here, at] = (
                query[here, at] * (long_part + skip_ref[0:1, at] * drive[here, at])
            ).astype(BF16)
        return carry

    for chunk in range(chunks):
        arrived(2, chunk, lt)
        lax.fori_loop(chunk * lines // 128, (chunk + 1) * lines // 128, finish, 0, unroll=True)

    edge.wait_send()
    for chunk in range(chunks):
        left(0, chunk, ht)
        left(1, chunk, dt)
        left(2, chunk, ys)


def solution(mesh):
    parts = mesh.shape["seq"]

    def on_device(qkv, short_weight, long_filter, skip):
        tok, chans = long_filter.shape
        rows, lines = parts * R, parts * C
        chunks = chans // lines
        f1, w, wi, g1, tw = tables(parts, tok)
        vmem = pl.BlockSpec(memory_space=pltpu.VMEM)
        hbm = pl.BlockSpec(memory_space=pl.ANY)
        return pl.pallas_call(
            functools.partial(kernel, parts),
            out_shape=pltpu.VMEM((tok, chans), BF16),
            in_specs=[hbm] * 9,
            out_specs=vmem,
            scratch_shapes=[
                pltpu.VMEM(short_weight.shape, F32),
                pltpu.VMEM((1, chans), F32),
                pltpu.VMEM(tw.shape, F32),
                pltpu.VMEM(qkv.shape, BF16),
                pltpu.VMEM((tok, chans), F32),
                pltpu.VMEM(f1.shape, BF16),
                pltpu.VMEM(w.shape, BF16),
                pltpu.VMEM(wi.shape, BF16),
                pltpu.VMEM(g1.shape, BF16),
                pltpu.VMEM((3, 16, chans), BF16),
                pltpu.VMEM((16, chans // 2), BF16),
                pltpu.VMEM((16, chans // 2), BF16),
                pltpu.VMEM((3, 8, chans), F32),
                pltpu.VMEM((chunks * rows, tok // 2), BF16),
                pltpu.VMEM((chunks * rows, tok // 2), BF16),
                pltpu.VMEM((chunks * rows, tok // 2), BF16),
                pltpu.VMEM((chunks * rows, tok // 2), BF16),
                pltpu.VMEM((chunks * rows, tok // 2), BF16),
                pltpu.VMEM((chunks * rows, tok // 2), BF16),
                pltpu.VMEM((tok, chans), F32),
                pltpu.VMEM((tok, chans), F32),
                pltpu.VMEM((lines, 2 * tok), F32),
                pltpu.VMEM((lines, 2 * tok), BF16),
                pltpu.VMEM((lines, 2 * tok), BF16),
                pltpu.VMEM((2 * rows, tok // 2), BF16),
                pltpu.SemaphoreType.DMA((chunks + 9,)),
                pltpu.SemaphoreType.DMA((2,)),
                pltpu.SemaphoreType.DMA((3, chunks)),
                pltpu.SemaphoreType.DMA((3, chunks)),
            ],
            compiler_params=pltpu.CompilerParams(
                collective_id=0, has_side_effects=True, vmem_limit_bytes=60 * 2**20
            ),
        )(qkv, short_weight, long_filter, skip[None, :], f1, w, wi, g1, tw)

    return jax.shard_map(
        on_device,
        mesh=mesh,
        in_specs=(P(None, "seq", "ch"), P(None, None, "ch"), P("seq", "ch"), P("ch")),
        out_specs=P("seq", "ch"),
        check_vma=False,
    )
```

```python
import functools

import jax
import jax.numpy as jnp
import numpy as np
from jax import lax
from jax.experimental import pallas as pl
from jax.experimental.pallas import tpu as pltpu
from jax.sharding import PartitionSpec as P

MESH = pl.DeviceIdType.MESH
C = 8
R = 16
STEPS = ((2, 2), (2, 1), (1, 2), (2, 3), (3, 2), (1, 1), (3, 3), (1, 3), (3, 1), (2, 0), (0, 2), (0, 1), (1, 0), (0, 3), (3, 0))
F32 = jnp.float32
BF16 = jnp.bfloat16


def dot(a, b):
    return jnp.dot(a, b, preferred_element_type=F32)


def tables(parts, tok):
    place = np.arange(parts)
    odd = 2 * place + 1
    angle = 2 * np.pi * np.outer(odd, place) / (4 * parts)
    spread = lambda m: np.kron(m, np.eye(R))
    f1 = np.concatenate([spread(np.cos(angle)), spread(-np.sin(angle))], axis=0)
    g1 = np.concatenate([spread(np.cos(angle).T), spread(-np.sin(angle).T)], axis=1)
    offset = np.arange(tok)
    angle = 2 * np.pi * (np.outer(offset, offset) % tok) / tok
    cos, sin = np.cos(angle), np.sin(angle)
    w = np.block([[cos, -sin], [sin, cos]])
    wi = np.block([[cos, sin], [-sin, cos]])
    angle = 2 * np.pi * np.outer(odd, offset) / (4 * parts * tok)
    tw = np.stack([np.cos(angle), np.sin(angle)])
    half = lambda m: m.astype(np.float32).astype(BF16)
    rest = lambda m: half(m - half(m).astype(np.float64))
    f1 = np.stack([half(f1), rest(f1)])
    g1 = np.stack([half(g1), rest(g1)])
    return f1, np.stack([half(w), rest(w)]), half(wi), g1, tw.astype(np.float32)


def kernel(
    parts, qkv_hbm, sw_hbm, filt_hbm, skip_hbm, f1_hbm, w_hbm, wi_hbm, g1_hbm, tw_hbm, o_ref,
    sw_ref, skip_ref, tw_ref, qkv, filt, f1, w, wi, g1, tail, ends, halo, ht, dt, hr, xr, ys, lt, drive, query, spec, b, y, g,
    load_sem, halo_sem, send_sem, recv_sem,
):
    me = lax.axis_index("seq")
    ch = lax.axis_index("ch")
    tok = qkv.shape[1]
    chans = qkv.shape[2]
    rows = parts * R
    lines = parts * C
    chunks = chans // lines
    half = tok // 2

    lanes = [pl.ds(chunk * lines, lines) for chunk in range(chunks)]
    loads = [
        pltpu.make_async_copy(src, dst, load_sem.at[i])
        for i, (src, dst) in enumerate(
            [(filt_hbm.at[:, at], filt.at[:, at]) for at in lanes]
            + [(qkv_hbm.at[:, pl.ds(tok - 16, 16), :], tail)]
            + [(qkv_hbm, qkv), (sw_hbm, sw_ref), (skip_hbm, skip_ref), (tw_hbm, tw_ref), (f1_hbm, f1), (w_hbm, w), (wi_hbm, wi), (g1_hbm, g1)]
        )
    ]

    barrier = pltpu.get_barrier_semaphore()

    z, x, core = me >> 3, (me >> 1) & 3, me & 1

    def tour(steps, visit, side=None):
        for flip in range(2):
            for some in (steps[:8], steps[8:]):
                code = sum((4 * dz + dx) << (4 * i) for i, (dz, dx) in enumerate(some))
                code = code - 2**32 if code >= 2**31 else code

                def one(k, carry):
                    step = (jnp.int32(code) >> (4 * k)) & 15
                    visit((((z + (step >> 2)) & 3) << 3) + (((x + step) & 3) << 1) + ((core ^ flip) if side is None else (side ^ flip)))
                    return carry

                lax.fori_loop(0, len(some), one, 0, unroll=True)
        visit(me ^ 1)

    def greet(to):
        pl.semaphore_signal(barrier, inc=1, device_id=(to, ch), device_id_type=MESH)

    tour(STEPS, greet)
    for load in loads[: chunks + 1]:
        load.start()

    def turn(dst, j, value):
        value = value.T
        for d in range(128 // C):
            mine = value[d * C : (d + 1) * C, :]
            message = jnp.concatenate([mine[:, :half], mine[:, half:]], axis=0).astype(BF16)
            dst[pl.ds(pl.multiple_of(j * 128 * R // C + d * R, R), R), :] = message

    def turn_filter(j, carry):
        turn(ht, j, filt[:, pl.ds(pl.multiple_of(j * 128, 128), 128)])
        return carry

    loads[0].wait()
    lax.fori_loop(0, lines // 128, turn_filter, 0)
    loads[chunks].wait()
    last = [tail[m].astype(F32)[14:, :] for m in range(3)]
    ends[...] = jnp.concatenate(last + [jnp.zeros((10, chans), F32)], axis=0).astype(BF16)
    pl.semaphore_wait(barrier, parts - 1)

    edge = pltpu.make_async_remote_copy(
        src_ref=ends, dst_ref=halo, send_sem=halo_sem.at[0], recv_sem=halo_sem.at[1],
        device_id=((me + 1) & (parts - 1), ch), device_id_type=MESH,
    )
    edge.start()

    def deal(kind, chunk, src, dst):
        base = chunk * rows

        def send(to):
            pltpu.make_async_remote_copy(
                src_ref=src.at[pl.ds(pl.multiple_of(base + to * R, R), R), :],
                dst_ref=dst.at[pl.ds(pl.multiple_of(base + me * R, R), R), :],
                send_sem=send_sem.at[kind, chunk],
                recv_sem=recv_sem.at[kind, chunk],
                device_id=(to, ch),
                device_id_type=MESH,
            ).start()

        tour(STEPS, send, 1 if kind == 2 else None)
        own = pl.ds(pl.multiple_of(base + me * R, R), R)
        pltpu.make_async_copy(src.at[own, :], dst.at[own, :], recv_sem.at[kind, chunk]).start()

    def arrived(kind, chunk, dst):
        whole = dst.at[pl.ds(pl.multiple_of(chunk * rows, rows), rows), :]
        pltpu.make_async_copy(whole, whole, recv_sem.at[kind, chunk]).wait()

    def left(kind, chunk, src):
        sent = src.at[pl.ds(0, rows - R), :]
        pltpu.make_async_copy(sent, sent, send_sem.at[kind, chunk]).wait()

    deal(0, 0, ht, hr)
    for load in loads[chunks + 1 :]:
        load.start()
    loads[chunks + 1].wait()
    loads[chunks + 2].wait()
    edge.wait_recv()
    first = jnp.where(me > 0, 1.0, 0.0).astype(F32)

    def short(m, at):
        before = halo[:, at].astype(F32)[2 * m : 2 * m + 2, :] * first
        before = jnp.concatenate([jnp.zeros((6, 128), F32), before], axis=0)
        ext = jnp.concatenate([before, qkv[m, :, at].astype(F32)], axis=0)
        return (
            sw_ref[m, 0:1, at] * ext[8:, :]
            + sw_ref[m, 1:2, at] * ext[7:-1, :]
            + sw_ref[m, 2:3, at] * ext[6:-2, :]
        )

    for chunk in range(chunks):

        def gate(j, carry):
            at = pl.ds(pl.multiple_of(j * 128, 128), 128)
            value = short(1, at) * short(2, at)
            drive[:, at] = value
            turn(dt, j, value)
            return carry

        if chunk:
            loads[chunk].wait()
            lax.fori_loop(chunk * lines // 128, (chunk + 1) * lines // 128, turn_filter, 0)
            deal(0, chunk, ht, hr)
        lax.fori_loop(chunk * lines // 128, (chunk + 1) * lines // 128, gate, 0)
        deal(1, chunk, dt, xr)

    loads[chunks + 3].wait()

    def ask(j, carry):
        at = pl.ds(pl.multiple_of(j * 128, 128), 128)
        asked = short(0, at)
        query[:, at] = asked
        drive[:, at] = asked * (skip_ref[0:1, at] * drive[:, at])
        return carry

    lax.fori_loop(0, chans // 128, ask, 0)

    def split(m_ref, at, value):
        return dot(m_ref[0, at, :], value) + dot(m_ref[1, at, :], value)

    def along_parts(blocks):
        real, imag = split(f1, slice(0, rows), blocks), split(f1, slice(rows, 2 * rows), blocks)
        for k in range(0, parts, 2):
            for n in range(2):
                at = slice(n * half, (n + 1) * half)
                turned = []
                for p in (k, k + 1):
                    cos, sin = tw_ref[0, p : p + 1, at], tw_ref[1, p : p + 1, at]
                    here = slice(p * R + n * C, p * R + (n + 1) * C)
                    re, im = real[here, :], imag[here, :]
                    turned.append((re * cos + im * sin, im * cos - re * sin))
                b[k * C : (k + 2) * C, n * half : (n + 1) * half] = jnp.concatenate(
                    [t[0] for t in turned], axis=0
                ).astype(BF16)
                b[k * C : (k + 2) * C, tok + n * half : tok + (n + 1) * half] = jnp.concatenate(
                    [t[1] for t in turned], axis=0
                ).astype(BF16)

    for load in loads[chunks + 4 :]:
        load.wait()

    def place(chunk):
        return pl.ds(pl.multiple_of(chunk * rows, rows), rows)

    def filter_spectra(chunk):
        arrived(0, chunk, hr)
        along_parts(hr[place(chunk), :])
        for n in range(4):
            spec[:, n * half : (n + 1) * half] = dot(b[...], w[0, :, n * half : (n + 1) * half]) + dot(b[...], w[1, :, n * half : (n + 1) * half])

    def convolve(chunk):
        arrived(1, chunk, xr)
        along_parts(xr[place(chunk), :])
        for n in range(2):
            real_at, imag_at = slice(n * half, (n + 1) * half), slice(tok + n * half, tok + (n + 1) * half)
            xre, xim = dot(b[...], w[0, :, real_at]), dot(b[...], w[0, :, imag_at])
            hre, him = spec[:, real_at], spec[:, imag_at]
            y[:, real_at] = (xre * hre - xim * him).astype(BF16)
            y[:, imag_at] = (xre * him + xim * hre).astype(BF16)
        back = [dot(y[...], wi[:, n * half : (n + 1) * half]) for n in range(4)]
        scale = 2.0 / (2 * parts * tok)
        for k in range(parts):
            turned = []
            for n in range(2):
                at = slice(n * half, (n + 1) * half)
                cos, sin = tw_ref[0, k : k + 1, at] * scale, tw_ref[1, k : k + 1, at] * scale
                re, im = back[n][k * C : (k + 1) * C, :], back[2 + n][k * C : (k + 1) * C, :]
                turned.append((re * cos - im * sin, im * cos + re * sin))
            for part in range(2):
                g[part * rows + k * R : part * rows + (k + 1) * R, :] = jnp.concatenate(
                    [t[part] for t in turned], axis=0
                ).astype(BF16)
        ys[place(chunk), :] = split(g1, slice(0, rows), g[...]).astype(BF16)

    def one_chunk(chunk, carry):
        filter_spectra(chunk)
        convolve(chunk)
        deal(2, chunk, ys, lt)
        return carry

    lax.fori_loop(0, chunks, one_chunk, 0)

    def finish(j, carry):
        at = pl.ds(pl.multiple_of(j * 128, 128), 128)
        came = lt[pl.ds(pl.multiple_of(j * 128 * R // C, 128 * R // C), 128 * R // C), :].astype(F32)
        for n in range(2):
            long_part = jnp.concatenate(
                [came[d * R + n * C : d * R + (n + 1) * C, :] for d in range(128 // C)], axis=0
            ).T
            here = slice(n * half, (n + 1) * half)
            o_ref[here, at] = (
                query[here, at] * long_part + drive[here, at]
            ).astype(BF16)
        return carry

    for chunk in range(chunks):
        arrived(2, chunk, lt)
        lax.fori_loop(chunk * lines // 128, (chunk + 1) * lines // 128, finish, 0)

    edge.wait_send()
    for chunk in range(chunks):
        left(0, chunk, ht)
        left(1, chunk, dt)
        left(2, chunk, ys)


def solution(mesh):
    parts = mesh.shape["seq"]

    def on_device(qkv, short_weight, long_filter, skip):
        tok, chans = long_filter.shape
        rows, lines = parts * R, parts * C
        chunks = chans // lines
        f1, w, wi, g1, tw = tables(parts, tok)
        vmem = pl.BlockSpec(memory_space=pltpu.VMEM)
        hbm = pl.BlockSpec(memory_space=pl.ANY)
        return pl.pallas_call(
            functools.partial(kernel, parts),
            out_shape=pltpu.VMEM((tok, chans), BF16),
            in_specs=[hbm] * 9,
            out_specs=vmem,
            scratch_shapes=[
                pltpu.VMEM(short_weight.shape, F32),
                pltpu.VMEM((1, chans), F32),
                pltpu.VMEM(tw.shape, F32),
                pltpu.VMEM(qkv.shape, BF16),
                pltpu.VMEM((tok, chans), F32),
                pltpu.VMEM(f1.shape, BF16),
                pltpu.VMEM(w.shape, BF16),
                pltpu.VMEM(wi.shape, BF16),
                pltpu.VMEM(g1.shape, BF16),
                pltpu.VMEM((3, 16, chans), BF16),
                pltpu.VMEM((16, chans), BF16),
                pltpu.VMEM((16, chans), BF16),
                pltpu.VMEM((chunks * rows, tok // 2), BF16),
                pltpu.VMEM((chunks * rows, tok // 2), BF16),
                pltpu.VMEM((chunks * rows, tok // 2), BF16),
                pltpu.VMEM((chunks * rows, tok // 2), BF16),
                pltpu.VMEM((chunks * rows, tok // 2), BF16),
                pltpu.VMEM((chunks * rows, tok // 2), BF16),
                pltpu.VMEM((tok, chans), F32),
                pltpu.VMEM((tok, chans), F32),
                pltpu.VMEM((lines, 2 * tok), F32),
                pltpu.VMEM((lines, 2 * tok), BF16),
                pltpu.VMEM((lines, 2 * tok), BF16),
                pltpu.VMEM((2 * rows, tok // 2), BF16),
                pltpu.SemaphoreType.DMA((chunks + 9,)),
                pltpu.SemaphoreType.DMA((2,)),
                pltpu.SemaphoreType.DMA((3, chunks)),
                pltpu.SemaphoreType.DMA((3, chunks)),
            ],
            compiler_params=pltpu.CompilerParams(
                collective_id=0, has_side_effects=True, vmem_limit_bytes=60 * 2**20
            ),
        )(qkv, short_weight, long_filter, skip[None, :], f1, w, wi, g1, tw)

    return jax.shard_map(
        on_device,
        mesh=mesh,
        in_specs=(P(None, "seq", "ch"), P(None, None, "ch"), P("seq", "ch"), P("ch")),
        out_specs=P("seq", "ch"),
        check_vma=False,
    )
```
